32 devices in a mesh: dp: 8 (over y, x, core), hd: 4 (over z).
Axes of the slice: x: 2, y: 2, z: 4, core: 2. Of those that a mesh axis runs over, the one named last changes fastest.
Arguments:
- query_nope: bfloat16 [512, 16384], P('dp', 'hd'), may hold values from -6 to 6
- query_rope: bfloat16 [512, 8192], P('dp', 'hd')
- latent: bfloat16 [512, 512], P('dp'), may hold values from -6 to 6
- key_rope: bfloat16 [512, 64], P('dp'), may hold values from -6 to 6
- key_up: bfloat16 [512, 16384], P(None, 'hd'), may hold values from -0.25 to 0.25
- value_up: bfloat16 [512, 16384], P(None, 'hd'), may hold values from -0.25 to 0.25
- output_weight: bfloat16 [16384, 7168], P('hd', 'dp'), may hold values from -0.046875 to 0.046875
- residual: bfloat16 [512, 7168], P('dp', 'hd'), may hold values from -6 to 6
- norm_gain: float32 [7168], P('hd'), may hold values from 0.1 to 1.9
- gate_weight: bfloat16 [7168, 18432], P('hd', 'dp'), may hold values from -0.0625 to 0.0625
- up_weight: bfloat16 [7168, 18432], P('hd', 'dp'), may hold values from -0.0625 to 0.0625
- down_weight: bfloat16 [18432, 7168], P('dp', 'hd'), may hold values from -0.046875 to 0.046875
- rank_tokens: int32 [8], replicated, may hold values from 1 to 64, 256 in all
- request_ids: int32 [8, 64], P('dp'), may hold values from 0 to 3, never falling along the last dimension, each value on 1 to 32 neighbouring positions
Outputs:
- layer_out: bfloat16 [512, 7168], P('dp', 'hd')
The draws below stay inside these ranges and needn't reach their ends.
Inputs may be any that keep to these rules, and one draw needn't show every extreme that they name: `rank_tokens`: the counts sum to 256. `request_ids`: along each rank's slots the number never falls; one request covers at most 32 slots.
All inputs are finite; a program needn't handle non-finite values.
Results may differ from the reference program's by a relative error of at most 0.0085.
Values may be sent and summed in bfloat16 or wider, within the bound.
A program may use at most 128 MiB of HBM per device.

```python
import math
import jax
import jax.numpy as jnp
import numpy as np
from jax import lax

D = 7168
FF = 18432
H = 128
NOPE = 128
ROPE = 64
VH = 128
KVR = 512
REQS = 4
SLOTS = 64
MOST = 32
NTOK = 512
LIVE = 256
N_DP = 8


def rope_base(key):
    total_rows = SLOTS * N_DP
    return jnp.clip(jax.random.normal(jax.random.fold_in(key, 11), (total_rows, ROPE), jnp.float32), -6.0, 6.0)


def draw_key_rope(key, part):
    return rope_base(key).astype(jnp.bfloat16)


def draw_query_rope(key, part):
    key = jax.random.fold_in(key, 5)
    total_rows = SLOTS * N_DP
    drawn = jnp.clip(jax.random.normal(jax.random.fold_in(key, 1), (total_rows, H, ROPE), jnp.float32), -6.0, 6.0)
    return drawn.reshape(total_rows, H * ROPE).astype(jnp.bfloat16)


def block_levels(rng, shape, split, smallest, top_value):
    level, own = 1.0, jax.random.fold_in(rng, 6)
    for dim, parts in split:
        heights = jnp.exp(jax.random.uniform(jax.random.fold_in(own, dim), (parts,), jnp.float32, smallest / len(split), top_value / len(split)))
        level = level * jnp.repeat(heights, shape[dim] // parts).reshape([-1 if axis == dim else 1 for axis in range(len(shape))])
    return level


def length_profile(number_of, total, bound, slope):
    portions = [(1 << 20) // math.isqrt(grade ** slope) + 1 for grade in range(2, number_of + 1)]
    surplus, given = total - bound - (number_of - 1), [1] * (number_of - 1)
    while surplus > 0:
        candidates = [i for i in range(number_of - 1) if given[i] < bound]
        pool, left = sum([portions[i] for i in candidates]), surplus
        for i in candidates:
            addition = min(bound - given[i], max(1, left * portions[i] // pool), surplus)
            given[i] = given[i] + addition
            surplus = surplus - addition
    return np.array([bound] + given)


def ragged_sizes(stream_key, number_of, total, most, lean):
    if number_of == 2:
        one = jax.random.randint(stream_key, (), max(1, total - most), min(most, total - 1) + 1)
        return jnp.stack([one, total - one])
    tallies = jnp.asarray(length_profile(number_of, total, most, lean), jnp.int32)
    couples = (number_of - 1) // 2
    source_of, sink = tallies[1:1 + 2 * couples:2], tallies[2:2 + 2 * couples:2]
    margin = jnp.minimum(source_of - 1, most - sink)
    moved = jax.random.randint(jax.random.fold_in(stream_key, 1), (couples,), 0, 1 << 20) % (margin + 1)
    tallies = tallies.at[1:1 + 2 * couples:2].set(source_of - moved).at[2:2 + 2 * couples:2].set(sink + moved)
    return tallies[jax.random.permutation(jax.random.fold_in(stream_key, 2), number_of)]


def gaussian(key, dims, width, limit, pieces=(), kind=jnp.bfloat16):
    values = jax.random.normal(key, dims, jnp.float32) * width
    if len(pieces) > 0:
        values = block_levels(key, dims, pieces, -0.22, 0.18) * values
    return jnp.clip(values, min=-limit, max=limit).astype(kind)


def setup_inputs(seed: int = 0) -> dict:
    keys = jax.random.split(jax.random.key(seed), 15)
    query_nope = gaussian(keys[0], (NTOK, H * NOPE), 1.0, 6.0, ((0, 8), (1, 4)))
    query_rope = draw_query_rope(jax.random.fold_in(keys[14], 71), 0)
    latent = gaussian(keys[2], (NTOK, KVR), 1.0, 6.0, ((0, 8),))
    key_rope = draw_key_rope(jax.random.fold_in(keys[14], 71), 0)
    key_up = gaussian(keys[4], (KVR, H * NOPE), KVR ** -0.5, 0.25, ((1, 4),))
    value_up = gaussian(keys[5], (KVR, H * VH), KVR ** -0.5, 0.25, ((1, 4),))
    output_weight = gaussian(keys[6], (H * VH, D), (H * VH) ** -0.5, 0.046875, ((0, 4), (1, 8)))
    residual = gaussian(keys[7], (NTOK, D), 1.0, 6.0, ((0, 8), (1, 4)))
    norm_gain = jnp.clip(1.0 + 0.18 * jax.random.normal(keys[8], (D,), jnp.float32), 0.1, 1.9)
    gate_weight = gaussian(keys[9], (D, FF), D ** -0.5, 0.0625, ((0, 4), (1, 8)))
    up_weight = gaussian(keys[10], (D, FF), D ** -0.5, 0.0625, ((0, 4), (1, 8)))
    down_weight = gaussian(keys[11], (FF, D), FF ** -0.5, 0.046875, ((0, 8), (1, 4)))
    rank_tokens = ragged_sizes(keys[12], N_DP, LIVE, SLOTS, 2).astype(jnp.int32)
    request_ids = jax.vmap(lambda own: jnp.searchsorted(jnp.cumsum(ragged_sizes(own, REQS, SLOTS, MOST, 1)), jnp.arange(SLOTS), side="right"))(jax.random.split(keys[13], N_DP)).reshape((N_DP, SLOTS)).astype(jnp.int32)
    return {"query_nope": query_nope, "query_rope": query_rope, "latent": latent, "key_rope": key_rope, "key_up": key_up, "value_up": value_up, "output_weight": output_weight, "residual": residual, "norm_gain": norm_gain, "gate_weight": gate_weight, "up_weight": up_weight, "down_weight": down_weight, "rank_tokens": rank_tokens, "request_ids": request_ids}


def attend(query_nope, query_rope, latent, key_rope, request_row, key_up, value_up):
    slots = latent.shape[0]
    heads = key_up.shape[1] // NOPE
    key_nope = jnp.dot(latent, key_up, preferred_element_type=jnp.float32).astype(jnp.bfloat16)
    values = jnp.dot(latent, value_up, preferred_element_type=jnp.float32).astype(jnp.bfloat16)
    query_heads = query_nope.reshape(slots, heads, NOPE).astype(jnp.float32)
    rotary_heads = query_rope.reshape(slots, heads, ROPE).astype(jnp.float32)
    key_heads = key_nope.reshape(slots, heads, NOPE).astype(jnp.float32)
    scores = jnp.einsum('shd,thd->hst', query_heads, key_heads)
    scores = scores + jnp.einsum('shd,td->hst', rotary_heads, key_rope.astype(jnp.float32))
    scores = scores * (NOPE + ROPE) ** (-0.5)
    position = jnp.arange(slots, dtype=jnp.int32)
    allowed = (request_row[:, None] == request_row[None, :]) & (position[None, :] <= position[:, None])
    scores = jnp.where(allowed[None, :, :], scores, jnp.float32(-1e+30))
    top = lax.optimization_barrier(jnp.max(scores, axis=-1, keepdims=True))
    raised = jnp.exp(scores - top)
    weights = (raised / lax.optimization_barrier(jnp.sum(raised, axis=-1, keepdims=True))).astype(jnp.bfloat16)
    value_heads = values.reshape(slots, heads, VH).astype(jnp.float32)
    attended = jnp.einsum('hst,thd->shd', weights.astype(jnp.float32), value_heads)
    return attended.astype(jnp.bfloat16).reshape(slots, heads * VH)

def reference(query_nope, query_rope, latent, key_rope, key_up, value_up, output_weight, residual, norm_gain, gate_weight, up_weight, down_weight, rank_tokens, request_ids):
    ranks = rank_tokens.shape[0]

    def one_rank(items):
        return attend(items[0], items[1], items[2], items[3], items[4], key_up, value_up)
    attended = lax.map(one_rank, (query_nope.reshape(ranks, SLOTS, -1), query_rope.reshape(ranks, SLOTS, -1), latent.reshape(ranks, SLOTS, -1), key_rope.reshape(ranks, SLOTS, -1), request_ids))
    attended = attended.reshape(NTOK, -1)
    projected = jnp.dot(attended, output_weight, preferred_element_type=jnp.float32)
    mixed = (residual.astype(jnp.float32) + projected).astype(jnp.bfloat16)
    widened = mixed.astype(jnp.float32)
    mean_square = lax.optimization_barrier(jnp.sum(widened * widened, axis=1, keepdims=True)) / D
    normed = (widened * lax.rsqrt(mean_square + 1e-06) * norm_gain).astype(jnp.bfloat16)
    gate = jnp.dot(normed, gate_weight, preferred_element_type=jnp.float32)
    up_value = jnp.dot(normed, up_weight, preferred_element_type=jnp.float32)
    hidden = (jax.nn.silu(gate) * up_value).astype(jnp.bfloat16)
    mlp = jnp.dot(hidden, down_weight, preferred_element_type=jnp.float32)
    row_index = jnp.arange(NTOK, dtype=jnp.int32)
    counts = rank_tokens[row_index // SLOTS]
    live = row_index % SLOTS < counts
    result = (widened + mlp).astype(jnp.bfloat16)
    return jnp.where(live[:, None], result, jnp.zeros_like(result))
```

```python
import functools

import jax
import jax.numpy as jnp
from jax import lax
from jax.experimental import pallas as pl
from jax.experimental.pallas import tpu as pltpu
from jax.sharding import PartitionSpec as P

NOPE = 128
ROPE = 64
VH = 128
MESH = pl.DeviceIdType.MESH


def attend(query_nope, query_rope, latent, key_rope, key_up, value_up, request_row):
    slots = latent.shape[0]
    heads = key_up.shape[1] // NOPE
    key_nope = jnp.dot(latent, key_up, preferred_element_type=jnp.float32).astype(jnp.bfloat16)
    values = jnp.dot(latent, value_up, preferred_element_type=jnp.float32).astype(jnp.bfloat16)
    query_heads = query_nope.reshape(slots, heads, NOPE)
    rotary_heads = query_rope.reshape(slots, heads, ROPE)
    scores = jnp.einsum(
        "shd,thd->hst",
        query_heads,
        key_nope.reshape(slots, heads, NOPE),
        preferred_element_type=jnp.float32,
    )
    scores = scores + jnp.einsum(
        "shd,td->hst", rotary_heads, key_rope, preferred_element_type=jnp.float32
    )
    scores = scores * (NOPE + ROPE) ** (-0.5)
    position = jnp.arange(slots, dtype=jnp.int32)
    allowed = (request_row[:, None] == request_row[None, :]) & (
        position[None, :] <= position[:, None]
    )
    scores = jnp.where(allowed[None, :, :], scores, jnp.float32(-1e30))
    top = jnp.max(scores, axis=-1, keepdims=True)
    raised = jnp.exp(scores - top)
    weights = (raised / jnp.sum(raised, axis=-1, keepdims=True)).astype(jnp.bfloat16)
    attended = jnp.einsum(
        "hst,thd->shd",
        weights,
        values.reshape(slots, heads, VH),
        preferred_element_type=jnp.float32,
    )
    return attended.astype(jnp.bfloat16).reshape(slots, heads * VH)


def f32_dot(a, b):
    return jnp.dot(a, b, preferred_element_type=jnp.float32)


def layer_kernel(
    n,
    m,
    att,
    res,
    gain,
    pack,
    unpack,
    wo_hbm,
    wg_hbm,
    wu_hbm,
    wd_hbm,
    out,
    wo,
    wg,
    wu,
    wd,
    gathered,
    packed,
    res_all,
    part,
    from_low,
    from_high,
    mixed,
    scaled,
    squares,
    squares_all,
    gu,
    gu_low,
    gu_high,
    hidden,
    y,
    y_pair,
    pair_in,
    y_own,
    chip_in,
    w_sem,
    own_sem,
    ag_ring_send,
    ag_pair_send,
    ag_recv,
    res_send,
    res_recv,
    line_send,
    line_low,
    line_high,
    bc_ring_send,
    bc_pair_send,
    bc_recv,
    sq_send,
    sq_recv,
    gu_send,
    gu_low_recv,
    gu_high_recv,
    hid_send_up,
    hid_send_down,
    hid_recv,
    pair_send,
    pair_recv,
    chip_send,
    chip_recv,
):
    i, j = lax.axis_index("dp"), lax.axis_index("hd")
    chips = n // 2
    chip, core = i // 2, lax.rem(i, 2)
    sibling = i + 1 - 2 * core
    side = 1
    while side * side < chips:
        side *= 2
    nb, rows, width = mixed.shape
    tiles = gu.shape[0]
    tile = gu.shape[2] // 2
    mine = rows // m
    quarters = from_low.shape[0]
    step_rows = rows // quarters
    half_f = packed.shape[2]
    slots = att.shape[1]

    def place(c):
        a, b = c // side, lax.rem(c, side)
        return a * side + b + lax.rem(a, 2) * (side - 1 - 2 * b)

    def chip_at(k):
        k = lax.rem(k + 2 * chips, chips)
        a, b = k // side, lax.rem(k, side)
        return a * side + b + lax.rem(a, 2) * (side - 1 - 2 * b)

    here = place(chip)
    after, before = 2 * chip_at(here + 1) + core, 2 * chip_at(here - 1) + core

    def send(src, dst, s_sem, r_sem, dp, hd):
        copy = pltpu.make_async_remote_copy(
            src_ref=src,
            dst_ref=dst,
            send_sem=s_sem,
            recv_sem=r_sem,
            device_id={"dp": dp, "hd": hd},
            device_id_type=MESH,
        )
        copy.start()

    def landed(ref, r_sem):
        pltpu.make_async_copy(ref, ref, r_sem).wait()

    loads = []
    for q, (a, b) in enumerate(((wo_hbm, wo), (wg_hbm, wg), (wu_hbm, wu), (wd_hbm, wd))):
        load = pltpu.make_async_copy(a, b, w_sem.at[q])
        load.start()
        loads.append(load)

    barrier = pltpu.get_barrier_semaphore()
    for d in range(1, n):
        pl.semaphore_signal(
            barrier, inc=1, device_id={"dp": lax.rem(i + d, n), "hd": j}, device_id_type=MESH
        )
    for d in range(1, m):
        pl.semaphore_signal(
            barrier, inc=1, device_id={"dp": i, "hd": lax.rem(j + d, m)}, device_id_type=MESH
        )
    pl.semaphore_wait(barrier, n + m - 2)

    for h in range(2):
        send(
            att.at[h],
            gathered.at[h, i],
            ag_ring_send.at[h, 0],
            ag_recv.at[h, i],
            (after, before)[h],
            j,
        )
    for h in range(2):
        send(att.at[h], gathered.at[h, i], ag_pair_send.at[h, 0], ag_recv.at[h, i], sibling, j)
        pltpu.make_async_copy(att.at[h], gathered.at[h, i], own_sem.at[h]).start()
    for b in range(nb):
        target = j * nb + b

        @pl.when(target != i)
        def _():
            send(res.at[b], res_all.at[i], res_send.at[b], res_recv.at[i], target, j)

        @pl.when(target == i)
        def _():
            pltpu.make_async_copy(res.at[b], res_all.at[i], res_send.at[b]).start()

    for step in range(1, chips):
        for h in range(2):
            block = 2 * chip_at(here - step if h == 0 else here + step) + core
            landed(gathered.at[h, block], ag_recv.at[h, block])
            if step < chips - 1:
                send(
                    gathered.at[h, block],
                    gathered.at[h, block],
                    ag_ring_send.at[h, step],
                    ag_recv.at[h, block],
                    (after, before)[h],
                    j,
                )
            send(
                gathered.at[h, block],
                gathered.at[h, block],
                ag_pair_send.at[h, step],
                ag_recv.at[h, block],
                sibling,
                j,
            )
    for h in range(2):
        pltpu.make_async_copy(att.at[h], gathered.at[h, i], own_sem.at[h]).wait()
        for c in range(chips):
            block = 2 * c + 1 - core
            landed(gathered.at[h, block], ag_recv.at[h, block])
    for h in range(2):
        packed[h] = f32_dot(pack[...], gathered[h].reshape(n * slots, half_f)).astype(jnp.bfloat16)
    loads[0].wait()
    part[...] = (
        f32_dot(packed[0], wo[:half_f, :]) + f32_dot(packed[1], wo[half_f:, :])
    ).astype(jnp.bfloat16)

    target = i // nb
    slot = lax.rem(i, nb)

    def bc_forward(b, q, source_chip):
        up = q < quarters // 2
        far = lax.rem((here - place(source_chip) if up else place(source_chip) - here) + chips, chips)

        @pl.when(far < chips - 1)
        def _():
            sl = mixed.at[b, pl.ds(q * step_rows, step_rows)]
            send(sl, sl, bc_ring_send.at[b // 2, q], bc_recv.at[b, q], after if up else before, j)

    @pl.when(j == target)
    def _():
        for k in range(n):
            @pl.when(k != i)
            def _():
                landed(res_all.at[k], res_recv.at[k])

        pltpu.make_async_copy(res.at[slot], res_all.at[i], res_send.at[slot]).wait()
        base = f32_dot(pack[...], res_all[...].reshape(n * slots, width))
        mixed[slot] = base.astype(jnp.bfloat16)

    for q in [x for p in range(quarters // 2) for x in (p, p + quarters // 2)]:
        sl = pl.ds(q * step_rows, step_rows)

        @pl.when(jnp.logical_and(j > 0, j <= target))
        def _():
            landed(from_low.at[q], line_low.at[q])

        @pl.when(jnp.logical_and(j < m - 1, j >= target))
        def _():
            landed(from_high.at[q], line_high.at[q])

        @pl.when(jnp.logical_and(j > 0, j < target))
        def _():
            part[sl] = (part[sl].astype(jnp.float32) + from_low[q].astype(jnp.float32)).astype(
                jnp.bfloat16
            )

        @pl.when(jnp.logical_and(j < m - 1, j > target))
        def _():
            part[sl] = (part[sl].astype(jnp.float32) + from_high[q].astype(jnp.float32)).astype(
                jnp.bfloat16
            )

        @pl.when(j < target)
        def _():
            send(part.at[sl], from_low.at[q], line_send.at[q], line_low.at[q], i, j + 1)

        @pl.when(j > target)
        def _():
            send(part.at[sl], from_high.at[q], line_send.at[q], line_high.at[q], i, j - 1)

        @pl.when(j == target)
        def _():
            total = mixed[slot, sl].astype(jnp.float32) + part[sl].astype(jnp.float32)
            mixed[slot, sl] = total.astype(jnp.bfloat16)

            @pl.when(j > 0)
            def _():
                mixed[slot, sl] = (
                    mixed[slot, sl].astype(jnp.float32) + from_low[q].astype(jnp.float32)
                ).astype(jnp.bfloat16)

            @pl.when(j < m - 1)
            def _():
                mixed[slot, sl] = (
                    mixed[slot, sl].astype(jnp.float32) + from_high[q].astype(jnp.float32)
                ).astype(jnp.bfloat16)

            bc_forward(slot, q, chip)
            view = mixed.at[slot, sl]
            send(view, view, bc_pair_send.at[slot // 2, q], bc_recv.at[slot, q], sibling, j)

    for q in [x for p in range(quarters // 2) for x in (p, p + quarters // 2)]:
        sl = pl.ds(q * step_rows, step_rows)
        for bb in range(nb // 2):
            b = 2 * bb + core
            source = (j * nb + b) // 2

            @pl.when(source != chip)
            def _():
                view = mixed.at[b, sl]
                landed(view, bc_recv.at[b, q])
                bc_forward(b, q, source)
                send(view, view, bc_pair_send.at[bb, q], bc_recv.at[b, q], sibling, j)

    for q in range(quarters):
        sl = pl.ds(q * step_rows, step_rows)
        for bb in range(nb // 2):
            b = 2 * bb + 1 - core
            landed(mixed.at[b, sl], bc_recv.at[b, q])

    total = jnp.zeros((rows, 1), jnp.float32)
    for b in range(nb):
        wide = mixed[b].astype(jnp.float32)
        scaled[b] = (wide * gain[b]).astype(jnp.bfloat16)
        total = total + jnp.sum(wide * wide, axis=1, keepdims=True)
    squares[...] = jnp.broadcast_to(total, squares.shape)
    for d in range(1, m):
        p = lax.rem(j + d, m)
        send(
            squares.at[pl.ds(p * mine, mine)],
            squares_all.at[j],
            sq_send.at[d],
            sq_recv.at[j],
            i,
            p,
        )
    loads[1].wait()
    loads[2].wait()
    for t in range(tiles):
        cols = slice(t * tile, (t + 1) * tile)
        gate = f32_dot(scaled[0], wg[:width, cols])
        up = f32_dot(scaled[0], wu[:width, cols])
        for b in range(1, nb):
            gate = gate + f32_dot(scaled[b], wg[b * width : (b + 1) * width, cols])
            up = up + f32_dot(scaled[b], wu[b * width : (b + 1) * width, cols])
        gu[t, :, :tile] = gate.astype(jnp.bfloat16)
        gu[t, :, tile:] = up.astype(jnp.bfloat16)
        if t == 0:
            pass

        for s in range(m - 1):
            p_up, p_down = m - 1 - s, s
            rows_up, rows_down = pl.ds(p_up * mine, mine), pl.ds(p_down * mine, mine)

            @pl.when(j < p_up)
            def _():
                @pl.when(j > 0)
                def _():
                    landed(gu_low.at[t, p_up], gu_low_recv.at[t, p_up])
                    gu[t, rows_up] = (
                        gu[t, rows_up].astype(jnp.float32) + gu_low[t, p_up].astype(jnp.float32)
                    ).astype(jnp.bfloat16)

                send(
                    gu.at[t, rows_up],
                    gu_low.at[t, p_up],
                    gu_send.at[t, p_up],
                    gu_low_recv.at[t, p_up],
                    i,
                    j + 1,
                )

            @pl.when(j > p_down)
            def _():
                @pl.when(j < m - 1)
                def _():
                    landed(gu_high.at[t, p_down], gu_high_recv.at[t, p_down])
                    gu[t, rows_down] = (
                        gu[t, rows_down].astype(jnp.float32)
                        + gu_high[t, p_down].astype(jnp.float32)
                    ).astype(jnp.bfloat16)

                send(
                    gu.at[t, rows_down],
                    gu_high.at[t, p_down],
                    gu_send.at[t, p_down],
                    gu_high_recv.at[t, p_down],
                    i,
                    j - 1,
                )

    own = pl.ds(pl.multiple_of(j * mine, mine), mine)
    square = squares[own, :1]
    for d in range(1, m):
        p = lax.rem(j + d, m)
        landed(squares_all.at[p], sq_recv.at[p])
        square = square + squares_all[p, :, :1]
    scale = lax.rsqrt(square / (m * nb * width) + 1e-06)
    for t in range(tiles):
        @pl.when(j > 0)
        def _():
            landed(gu_low.at[t, j], gu_low_recv.at[t, j])
            gu[t, own] = (
                gu[t, own].astype(jnp.float32) + gu_low[t, j].astype(jnp.float32)
            ).astype(jnp.bfloat16)

        @pl.when(j < m - 1)
        def _():
            landed(gu_high.at[t, j], gu_high_recv.at[t, j])
            gu[t, own] = (
                gu[t, own].astype(jnp.float32) + gu_high[t, j].astype(jnp.float32)
            ).astype(jnp.bfloat16)

        gate = gu[t, own, :tile].astype(jnp.float32) * scale
        up = gu[t, own, tile:].astype(jnp.float32) * scale
        hidden[t, j] = (gate / (1.0 + jnp.exp(-gate)) * up).astype(jnp.bfloat16)

        view = hidden.at[t, j]

        @pl.when(j < m - 1)
        def _():
            send(view, view, hid_send_up.at[t, j], hid_recv.at[t, j], i, j + 1)

        @pl.when(j > 0)
        def _():
            send(view, view, hid_send_down.at[t, j], hid_recv.at[t, j], i, j - 1)

    for s in range(1, m):
        for t in range(tiles):
            @pl.when(j >= s)
            def _():
                view = hidden.at[t, j - s]
                landed(view, hid_recv.at[t, j - s])

                @pl.when(j < m - 1)
                def _():
                    send(view, view, hid_send_up.at[t, j - s], hid_recv.at[t, j - s], i, j + 1)

            @pl.when(j + s <= m - 1)
            def _():
                view = hidden.at[t, j + s]
                landed(view, hid_recv.at[t, j + s])

                @pl.when(j > 0)
                def _():
                    send(view, view, hid_send_down.at[t, j + s], hid_recv.at[t, j + s], i, j - 1)

    loads[3].wait()
    total = f32_dot(hidden[0].reshape(rows, tile), wd[:tile, :])
    for t in range(1, tiles):
        total = total + f32_dot(hidden[t].reshape(rows, tile), wd[t * tile : (t + 1) * tile, :])
    y[...] = total.astype(jnp.bfloat16)

    for d in range(chips):
        c = lax.rem(chip + d + 1, chips)
        y_pair[c] = f32_dot(unpack[2 * c + 1 - core], y[...]).astype(jnp.bfloat16)
        send(y_pair.at[c], pair_in.at[c], pair_send.at[c], pair_recv.at[c], sibling, j)
    for d in range(chips):
        c = lax.rem(chip + d + 1, chips)
        mine_rows = f32_dot(unpack[2 * c + core], y[...])
        landed(pair_in.at[c], pair_recv.at[c])
        y_own[c] = (mine_rows + pair_in[c].astype(jnp.float32)).astype(jnp.bfloat16)
        if d < chips - 1:
            send(
                y_own.at[c], chip_in.at[chip], chip_send.at[c], chip_recv.at[chip], 2 * c + core, j
            )
    kept = jnp.concatenate([f32_dot(unpack[i], mixed[b]) for b in range(nb)], axis=1)
    kept = kept + y_own[chip].astype(jnp.float32)
    for d in range(1, chips):
        c = lax.rem(chip + d, chips)
        landed(chip_in.at[c], chip_recv.at[c])
        kept = kept + chip_in[c].astype(jnp.float32)
    out[...] = kept.astype(jnp.bfloat16)

    def sent(ref, sem):
        pltpu.make_async_copy(ref, ref, sem).wait()

    for h in range(2):
        for step in range(chips):
            if step < chips - 1:
                sent(att.at[h], ag_ring_send.at[h, step])
            sent(att.at[h], ag_pair_send.at[h, step])
    for b in range(nb):
        @pl.when(j * nb + b != i)
        def _():
            sent(res.at[b], res_send.at[b])
    for q in range(quarters):
        @pl.when(j != target)
        def _():
            sent(from_low.at[q], line_send.at[q])

        for bb in range(nb // 2):
            source = (j * nb + 2 * bb + core) // 2
            up = q < quarters // 2
            far = lax.rem((here - place(source) if up else place(source) - here) + chips, chips)

            @pl.when(far < chips - 1)
            def _():
                sent(from_low.at[q], bc_ring_send.at[bb, q])

            sent(from_low.at[q], bc_pair_send.at[bb, q])
    for d in range(1, m):
        sent(squares_all.at[0], sq_send.at[d])
    for t in range(tiles):
        for p in range(m):
            @pl.when(p != j)
            def _():
                sent(gu_low.at[t, p], gu_send.at[t, p])

            @pl.when(jnp.logical_and(p <= j, j < m - 1))
            def _():
                sent(hidden.at[t, p], hid_send_up.at[t, p])

            @pl.when(jnp.logical_and(p >= j, j > 0))
            def _():
                sent(hidden.at[t, p], hid_send_down.at[t, p])
    for c in range(chips):
        sent(y_pair.at[c], pair_send.at[c])

        @pl.when(c != chip)
        def _():
            sent(y_own.at[c], chip_send.at[c])


def rest(att, res, gain, pack, unpack, wo, wg, wu, wd):
    n, m = lax.axis_size("dp"), lax.axis_size("hd")
    _, slots, half_f = att.shape
    nb, _, width = res.shape
    rows = pack.shape[0]
    features = wd.shape[1]
    units = wd.shape[0]
    tiles = 3 if units % 384 == 0 else 1
    tile = units // tiles
    quarters = 4
    chips = n // 2
    mine = rows // m
    bf, f32 = jnp.bfloat16, jnp.float32
    vmem = pl.BlockSpec(memory_space=pltpu.VMEM)
    hbm = pl.BlockSpec(memory_space=pl.ANY)
    dma = pltpu.SemaphoreType.DMA
    step_rows = rows // quarters
    scratch = [
        pltpu.VMEM(wo.shape, bf),
        pltpu.VMEM(wg.shape, bf),
        pltpu.VMEM(wu.shape, bf),
        pltpu.VMEM(wd.shape, bf),
        pltpu.VMEM((2, n, slots, half_f), bf),
        pltpu.VMEM((2, rows, half_f), bf),
        pltpu.VMEM((n, slots, width), bf),
        pltpu.VMEM((rows, width), bf),
        pltpu.VMEM((quarters, step_rows, width), bf),
        pltpu.VMEM((quarters, step_rows, width), bf),
        pltpu.VMEM((nb, rows, width), bf),
        pltpu.VMEM((nb, rows, width), bf),
        pltpu.VMEM((rows, 128), f32),
        pltpu.VMEM((m, mine, 128), f32),
        pltpu.VMEM((tiles, rows, 2 * tile), bf),
        pltpu.VMEM((tiles, m, mine, 2 * tile), bf),
        pltpu.VMEM((tiles, m, mine, 2 * tile), bf),
        pltpu.VMEM((tiles, m, mine, tile), bf),
        pltpu.VMEM((rows, features), bf),
        pltpu.VMEM((chips, slots, features), bf),
        pltpu.VMEM((chips, slots, features), bf),
        pltpu.VMEM((chips, slots, features), bf),
        pltpu.VMEM((chips, slots, features), bf),
        dma((4,)),
        dma((2,)),
        dma((2, chips)),
        dma((2, chips)),
        dma((2, n)),
        dma((nb,)),
        dma((n,)),
        dma((quarters,)),
        dma((quarters,)),
        dma((quarters,)),
        dma((nb // 2, quarters)),
        dma((nb // 2, quarters)),
        dma((nb, quarters)),
        dma((m,)),
        dma((m,)),
        dma((tiles, m)),
        dma((tiles, m)),
        dma((tiles, m)),
        dma((tiles, m)),
        dma((tiles, m)),
        dma((tiles, m)),
        dma((chips,)),
        dma((chips,)),
        dma((chips,)),
        dma((chips,)),
    ]
    return pl.pallas_call(
        functools.partial(layer_kernel, n, m),
        out_shape=jax.ShapeDtypeStruct((slots, features), bf),
        in_specs=[vmem] * 5 + [hbm] * 4,
        out_specs=vmem,
        scratch_shapes=scratch,
        compiler_params=pltpu.CompilerParams(
            collective_id=0, has_side_effects=True, vmem_limit_bytes=60 * 1024 * 1024
        ),
        cost_estimate=pl.CostEstimate(
            flops=2 * rows * (wo.size + wg.size + wu.size + wd.size),
            bytes_accessed=2 * (wo.size + wg.size + wu.size + wd.size),
            transcendentals=0,
        ),
    )(att, res, gain, pack, unpack, wo, wg, wu, wd)


def on_device(
    query_nope,
    query_rope,
    latent,
    key_rope,
    key_up,
    value_up,
    output_weight,
    residual,
    norm_gain,
    gate_weight,
    up_weight,
    down_weight,
    rank_tokens,
    request_ids,
):
    slots = latent.shape[0]
    n, m = lax.axis_size("dp"), lax.axis_size("hd")
    nb = n // m
    attended = attend(query_nope, query_rope, latent, key_rope, key_up, value_up, request_ids[0])
    att = attended.reshape(slots, 2, -1).transpose(1, 0, 2)
    res = residual.reshape(slots, nb, -1).transpose(1, 0, 2)
    gain = norm_gain.reshape(nb, 1, -1)
    rows = n * slots // 2
    first = jnp.cumsum(rank_tokens) - rank_tokens
    slot = jnp.arange(slots, dtype=jnp.int32)
    packed_row = jnp.where(
        slot[None, :] < rank_tokens[:, None], first[:, None] + slot[None, :], -1
    )
    row = jnp.arange(rows, dtype=jnp.int32)
    pack = (row[:, None] == packed_row.reshape(1, -1)).astype(jnp.bfloat16)
    unpack = (packed_row[:, :, None] == row[None, None, :]).astype(jnp.bfloat16)
    return rest(
        att, res, gain, pack, unpack, output_weight, gate_weight, up_weight, down_weight
    )


def solution(mesh):
    in_specs = (
        P("dp", "hd"),
        P("dp", "hd"),
        P("dp", None),
        P("dp", None),
        P(None, "hd"),
        P(None, "hd"),
        P("hd", "dp"),
        P("dp", "hd"),
        P("hd"),
        P("hd", "dp"),
        P("hd", "dp"),
        P("dp", "hd"),
        P(),
        P("dp", None),
    )
    out_specs = P("dp", "hd")
    return jax.shard_map(
        on_device, mesh=mesh, in_specs=in_specs, out_specs=out_specs, check_vma=False
    )
```

```python
import functools

import jax
import jax.numpy as jnp
from jax import lax
from jax.experimental import pallas as pl
from jax.experimental.pallas import tpu as pltpu
from jax.sharding import PartitionSpec as P

NOPE = 128
ROPE = 64
VH = 128
MESH = pl.DeviceIdType.MESH


def attend(query_nope, query_rope, latent, key_rope, key_up, value_up, request_row):
    slots = latent.shape[0]
    heads = key_up.shape[1] // NOPE
    key_nope = jnp.dot(latent, key_up, preferred_element_type=jnp.float32).astype(jnp.bfloat16)
    values = jnp.dot(latent, value_up, preferred_element_type=jnp.float32).astype(jnp.bfloat16)
    query_heads = query_nope.reshape(slots, heads, NOPE)
    rotary_heads = query_rope.reshape(slots, heads, ROPE)
    scores = jnp.einsum(
        "shd,thd->hst",
        query_heads,
        key_nope.reshape(slots, heads, NOPE),
        preferred_element_type=jnp.float32,
    )
    scores = scores + jnp.einsum(
        "shd,td->hst", rotary_heads, key_rope, preferred_element_type=jnp.float32
    )
    scores = scores * (NOPE + ROPE) ** (-0.5)
    position = jnp.arange(slots, dtype=jnp.int32)
    allowed = (request_row[:, None] == request_row[None, :]) & (
        position[None, :] <= position[:, None]
    )
    scores = jnp.where(allowed[None, :, :], scores, jnp.float32(-1e30))
    top = jnp.max(scores, axis=-1, keepdims=True)
    raised = jnp.exp(scores - top)
    weights = (raised / jnp.sum(raised, axis=-1, keepdims=True)).astype(jnp.bfloat16)
    attended = jnp.einsum(
        "hst,thd->shd",
        weights,
        values.reshape(slots, heads, VH),
        preferred_element_type=jnp.float32,
    )
    return attended.astype(jnp.bfloat16).reshape(slots, heads * VH)


def f32_dot(a, b):
    return jnp.dot(a, b, preferred_element_type=jnp.float32)


def layer_kernel(
    n,
    m,
    att,
    res,
    gain,
    pack,
    unpack,
    wo_hbm,
    wg_hbm,
    wu_hbm,
    wd_hbm,
    out,
    wo,
    wg,
    wu,
    wd,
    gathered,
    acc,
    res_all,
    part,
    from_low,
    from_high,
    mixed,
    scaled,
    squares,
    squares_all,
    gu,
    gu_in,
    hidden,
    y,
    y_pair,
    pair_in,
    y_own,
    chip_in,
    w_sem,
    own_sem,
    ag_ring_send,
    ag_pair_send,
    ag_recv,
    res_send,
    res_recv,
    line_send,
    line_low,
    line_high,
    bc_ring_send,
    bc_pair_send,
    bc_recv,
    sq_send,
    sq_recv,
    gu_send,
    gu_recv,
    hid_send_up,
    hid_send_down,
    hid_recv,
    pair_send,
    pair_recv,
    chip_send,
    chip_recv,
):
    i, j = lax.axis_index("dp"), lax.axis_index("hd")
    chips = n // 2
    chip, core = i // 2, lax.rem(i, 2)
    sibling = i + 1 - 2 * core
    side = 1
    while side * side < chips:
        side *= 2
    nb, rows, width = mixed.shape
    tiles = gu.shape[0]
    tile = gu.shape[3] // 2
    mine = rows // m
    quarters = from_low.shape[0]
    step_rows = rows // quarters
    half_f = gathered.shape[3]
    slots = att.shape[0]

    def att_half(h):
        return att.at[:, pl.ds(h * half_f, half_f)]

    def res_block(b):
        return res.at[:, pl.ds(b * width, width)] if len(res.shape) == 2 else res.at[b]

    def place(c):
        a, b = c // side, lax.rem(c, side)
        return a * side + b + lax.rem(a, 2) * (side - 1 - 2 * b)

    def chip_at(k):
        k = lax.rem(k + 2 * chips, chips)
        a, b = k // side, lax.rem(k, side)
        return a * side + b + lax.rem(a, 2) * (side - 1 - 2 * b)

    here = place(chip)
    after, before = 2 * chip_at(here + 1) + core, 2 * chip_at(here - 1) + core

    def send(src, dst, s_sem, r_sem, dp, hd):
        copy = pltpu.make_async_remote_copy(
            src_ref=src,
            dst_ref=dst,
            send_sem=s_sem,
            recv_sem=r_sem,
            device_id={"dp": dp, "hd": hd},
            device_id_type=MESH,
        )
        copy.start()

    def landed(ref, r_sem):
        pltpu.make_async_copy(ref, ref, r_sem).wait()

    loads = []
    for q, (a, b) in enumerate(((wo_hbm, wo), (wg_hbm, wg), (wu_hbm, wu), (wd_hbm, wd))):
        load = pltpu.make_async_copy(a, b, w_sem.at[q])
        if q == 0:
            load.start()
        loads.append(load)
    from_low[...] = jnp.zeros_like(from_low)
    from_high[...] = jnp.zeros_like(from_high)

    barrier = pltpu.get_barrier_semaphore()
    for d in range(1, n):
        pl.semaphore_signal(
            barrier, inc=1, device_id={"dp": lax.rem(i + d, n), "hd": j}, device_id_type=MESH
        )
    for d in range(1, m):
        pl.semaphore_signal(
            barrier, inc=1, device_id={"dp": i, "hd": lax.rem(j + d, m)}, device_id_type=MESH
        )
    pl.semaphore_wait(barrier, n + m - 2)

    for h in range(2):
        send(
            att_half(h),
            gathered.at[h, i],
            ag_ring_send.at[h, 0],
            ag_recv.at[h, i],
            (after, before)[h],
            j,
        )
    for h in range(2):
        send(att_half(h), gathered.at[h, i], ag_pair_send.at[h, 0], ag_recv.at[h, i], sibling, j)
        pltpu.make_async_copy(att_half(h), gathered.at[h, i], own_sem.at[h]).start()
    loads[0].wait()
    for load in loads[1:]:
        load.start()
    for step in range(chips):
        sources = [chip_at(here - step), chip_at(here + step)]
        for h in range(2):
            block = 2 * sources[h] + core
            if step == 0:
                pltpu.make_async_copy(att_half(h), gathered.at[h, i], own_sem.at[h]).wait()
                continue
            landed(gathered.at[h, block], ag_recv.at[h, block])
            view = gathered.at[h, block]
            if step < chips - 1:
                send(
                    view,
                    view,
                    ag_ring_send.at[h, step],
                    ag_recv.at[h, block],
                    (after, before)[h],
                    j,
                )
            send(view, view, ag_pair_send.at[h, step], ag_recv.at[h, block], sibling, j)
        if step == chips - 1:
            for b in range(nb):
                goal = j * nb + b

                @pl.when(goal != i)
                def _():
                    send(res_block(b), res_all.at[i], res_send.at[b], res_recv.at[i], goal, j)

                @pl.when(goal == i)
                def _():
                    pltpu.make_async_copy(res_block(b), res_all.at[i], res_send.at[b]).start()

        for h in range(2):
            block = 2 * sources[h] + 1 - core
            landed(gathered.at[h, block], ag_recv.at[h, block])
            both = gathered[h, pl.ds(2 * sources[h], 2)].reshape(2 * slots, half_f)
            sl = pl.ds(pl.multiple_of(2 * sources[h] * slots, 2 * slots), 2 * slots)
            term = f32_dot(both, wo[h * half_f : (h + 1) * half_f, :])
            first = step == 0 and h == 0 or step > 0 and 2 * step < chips
            first = first or (2 * step == chips and h == 0)
            acc[sl] = term if first else acc[sl] + term
    part[...] = f32_dot(pack[...], acc[...].astype(jnp.bfloat16)).astype(jnp.bfloat16)

    target = i // nb
    slot = lax.rem(i, nb)

    def bc_forward(b, q, source_chip):
        up = q < quarters // 2
        far = lax.rem((here - place(source_chip) if up else place(source_chip) - here) + chips, chips)

        @pl.when(far < chips - 1)
        def _():
            sl = mixed.at[b, pl.ds(q * step_rows, step_rows)]
            send(sl, sl, bc_ring_send.at[b // 2, q], bc_recv.at[b, q], after if up else before, j)

    @pl.when(j == target)
    def _():
        for k in range(n):
            @pl.when(k != i)
            def _():
                landed(res_all.at[k], res_recv.at[k])

        pltpu.make_async_copy(res_all.at[i], res_all.at[i], res_send.at[slot]).wait()
        base = f32_dot(pack[...], res_all[...].reshape(n * slots, width))
        mixed[slot] = base.astype(jnp.bfloat16)

    for q in [x for p in range(quarters // 2) for x in (p, p + quarters // 2)]:
        sl = pl.ds(q * step_rows, step_rows)

        @pl.when(jnp.logical_and(j > 0, j <= target))
        def _():
            landed(from_low.at[q], line_low.at[q])

        @pl.when(jnp.logical_and(j < m - 1, j >= target))
        def _():
            landed(from_high.at[q], line_high.at[q])

        @pl.when(jnp.logical_and(j > 0, j < target))
        def _():
            part[sl] = (part[sl].astype(jnp.float32) + from_low[q].astype(jnp.float32)).astype(
                jnp.bfloat16
            )

        @pl.when(jnp.logical_and(j < m - 1, j > target))
        def _():
            part[sl] = (part[sl].astype(jnp.float32) + from_high[q].astype(jnp.float32)).astype(
                jnp.bfloat16
            )

        @pl.when(j < target)
        def _():
            send(part.at[sl], from_low.at[q], line_send.at[q], line_low.at[q], i, j + 1)

        @pl.when(j > target)
        def _():
            send(part.at[sl], from_high.at[q], line_send.at[q], line_high.at[q], i, j - 1)

        @pl.when(j == target)
        def _():
            total = mixed[slot, sl].astype(jnp.float32) + part[sl].astype(jnp.float32)
            total = total + (from_low[q].astype(jnp.float32) + from_high[q].astype(jnp.float32))
            mixed[slot, sl] = total.astype(jnp.bfloat16)
            bc_forward(slot, q, chip)
            view = mixed.at[slot, sl]
            send(view, view, bc_pair_send.at[slot // 2, q], bc_recv.at[slot, q], sibling, j)

    for q in [x for p in range(quarters // 2) for x in (p, p + quarters // 2)]:
        sl = pl.ds(q * step_rows, step_rows)
        for bb in range(nb // 2):
            b = 2 * bb + core
            source = (j * nb + b) // 2

            @pl.when(source != chip)
            def _():
                view = mixed.at[b, sl]
                landed(view, bc_recv.at[b, q])
                bc_forward(b, q, source)
                send(view, view, bc_pair_send.at[bb, q], bc_recv.at[b, q], sibling, j)

    for q in range(quarters):
        sl = pl.ds(q * step_rows, step_rows)
        for bb in range(nb // 2):
            b = 2 * bb + 1 - core
            landed(mixed.at[b, sl], bc_recv.at[b, q])

    total = jnp.zeros((rows, 1), jnp.float32)
    for b in range(nb):
        wide = mixed[b].astype(jnp.float32)
        scaled[b] = (wide * gain[:, b * width : (b + 1) * width]).astype(jnp.bfloat16)
        total = total + jnp.sum(wide * wide, axis=1, keepdims=True)
    squares[...] = jnp.broadcast_to(total, squares.shape)
    for d in range(1, m):
        p = lax.rem(j + d, m)
        send(
            squares.at[pl.ds(p * mine, mine)],
            squares_all.at[j],
            sq_send.at[d],
            sq_recv.at[j],
            i,
            p,
        )
    loads[1].wait()
    loads[2].wait()
    for t in range(tiles):
        @pl.when(j == 0)
        def _():
            gu_in[0, t, 0] = jnp.zeros_like(gu_in[0, t, 0])

        @pl.when(j == m - 1)
        def _():
            gu_in[1, t, m - 1] = jnp.zeros_like(gu_in[1, t, m - 1])

    def gate_up(t):
        cols = slice(t * tile, (t + 1) * tile)
        gate = f32_dot(scaled[0], wg[:width, cols])
        up = f32_dot(scaled[0], wu[:width, cols])
        for b in range(1, nb):
            gate = gate + f32_dot(scaled[b], wg[b * width : (b + 1) * width, cols])
            up = up + f32_dot(scaled[b], wu[b * width : (b + 1) * width, cols])
        gu[t, :, :, :tile] = gate.astype(jnp.bfloat16).reshape(m, mine, tile)
        gu[t, :, :, tile:] = up.astype(jnp.bfloat16).reshape(m, mine, tile)

    def pass_sums(t):
        for s in range(m - 1):
            for turn in range(2):
                nearer = (2 * j) // m
                way = nearer if turn == 0 else 1 - nearer
                p = (1 - way) * (m - 1 - s) + way * s
                ahead = 1 - 2 * way
                come = (1 - way) * j + way * (m - 1 - j)

                @pl.when((p - j) * ahead > 0)
                def _():
                    @pl.when(come > 0)
                    def _():
                        landed(gu_in.at[way, t, p], gu_recv.at[way, t, p])
                        gu[t, p] = (
                            gu[t, p].astype(jnp.float32) + gu_in[way, t, p].astype(jnp.float32)
                        ).astype(jnp.bfloat16)

                    send(
                        gu.at[t, p],
                        gu_in.at[way, t, p],
                        gu_send.at[t, p],
                        gu_recv.at[way, t, p],
                        i,
                        j + ahead,
                    )

    def row_scale():
        square = squares[pl.ds(pl.multiple_of(j * mine, mine), mine), :1]
        for d in range(1, m):
            p = lax.rem(j + d, m)
            landed(squares_all.at[p], sq_recv.at[p])
            square = square + squares_all[p, :, :1]
        return lax.rsqrt(square / (m * nb * width) + 1e-06)

    def own_hidden(t, scale):
        @pl.when(j > 0)
        def _():
            landed(gu_in.at[0, t, j], gu_recv.at[0, t, j])

        @pl.when(j < m - 1)
        def _():
            landed(gu_in.at[1, t, j], gu_recv.at[1, t, j])

        total = gu[t, j].astype(jnp.float32) + (
            gu_in[0, t, j].astype(jnp.float32) + gu_in[1, t, j].astype(jnp.float32)
        )
        gate, up = total[:, :tile] * scale, total[:, tile:] * scale
        hidden[t, j] = (gate / (1.0 + jnp.exp(-gate)) * up).astype(jnp.bfloat16)
        view = hidden.at[t, j]

        @pl.when(j < m - 1)
        def _():
            send(view, view, hid_send_up.at[t, j], hid_recv.at[t, j], i, j + 1)

        @pl.when(j > 0)
        def _():
            send(view, view, hid_send_down.at[t, j], hid_recv.at[t, j], i, j - 1)

    def pass_hidden(t):
        for s in range(1, m):
            @pl.when(j >= s)
            def _():
                view = hidden.at[t, j - s]
                landed(view, hid_recv.at[t, j - s])

                @pl.when(j < m - 1)
                def _():
                    send(view, view, hid_send_up.at[t, j - s], hid_recv.at[t, j - s], i, j + 1)

            @pl.when(j + s <= m - 1)
            def _():
                view = hidden.at[t, j + s]
                landed(view, hid_recv.at[t, j + s])

                @pl.when(j > 0)
                def _():
                    send(view, view, hid_send_down.at[t, j + s], hid_recv.at[t, j + s], i, j - 1)

    for t in range(tiles + 2):
        if t < tiles:
            gate_up(t)
            pass_sums(t)
        if t == 0:
            scale = row_scale()
        if 1 <= t <= tiles:
            own_hidden(t - 1, scale)
        if t >= 2:
            pass_hidden(t - 2)

    loads[3].wait()
    total = f32_dot(hidden[0].reshape(rows, tile), wd[:tile, :])
    for t in range(1, tiles):
        total = total + f32_dot(hidden[t].reshape(rows, tile), wd[t * tile : (t + 1) * tile, :])
    y[...] = total.astype(jnp.bfloat16)

    for d in range(chips):
        c = lax.rem(chip + d + 1, chips)
        y_pair[c] = f32_dot(unpack[2 * c + 1 - core], y[...]).astype(jnp.bfloat16)
        send(y_pair.at[c], pair_in.at[c], pair_send.at[c], pair_recv.at[c], sibling, j)
    for d in range(chips):
        c = lax.rem(chip + d + 1, chips)
        mine_rows = f32_dot(unpack[2 * c + core], y[...])
        landed(pair_in.at[c], pair_recv.at[c])
        y_own[c] = (mine_rows + pair_in[c].astype(jnp.float32)).astype(jnp.bfloat16)
        if d < chips - 1:
            send(
                y_own.at[c], chip_in.at[chip], chip_send.at[c], chip_recv.at[chip], 2 * c + core, j
            )
    kept = jnp.concatenate([f32_dot(unpack[i], mixed[b]) for b in range(nb)], axis=1)
    kept = kept + y_own[chip].astype(jnp.float32)
    for d in range(1, chips):
        c = lax.rem(chip + d, chips)
        landed(chip_in.at[c], chip_recv.at[c])
        kept = kept + chip_in[c].astype(jnp.float32)
    out[...] = kept.astype(jnp.bfloat16)

    def sent(ref, sem):
        pltpu.make_async_copy(ref, ref, sem).wait()

    for h in range(2):
        for step in range(chips):
            if step < chips - 1:
                sent(gathered.at[h, 0], ag_ring_send.at[h, step])
            sent(gathered.at[h, 0], ag_pair_send.at[h, step])
    for b in range(nb):
        @pl.when(j * nb + b != i)
        def _():
            sent(res_all.at[0], res_send.at[b])
    for q in range(quarters):
        @pl.when(j != target)
        def _():
            sent(from_low.at[q], line_send.at[q])

        for bb in range(nb // 2):
            source = (j * nb + 2 * bb + core) // 2
            up = q < quarters // 2
            far = lax.rem((here - place(source) if up else place(source) - here) + chips, chips)

            @pl.when(far < chips - 1)
            def _():
                sent(from_low.at[q], bc_ring_send.at[bb, q])

            sent(from_low.at[q], bc_pair_send.at[bb, q])
    for d in range(1, m):
        sent(squares_all.at[0], sq_send.at[d])
    for t in range(tiles):
        for p in range(m):
            @pl.when(p != j)
            def _():
                sent(gu.at[t, p], gu_send.at[t, p])

            @pl.when(jnp.logical_and(p <= j, j < m - 1))
            def _():
                sent(hidden.at[t, p], hid_send_up.at[t, p])

            @pl.when(jnp.logical_and(p >= j, j > 0))
            def _():
                sent(hidden.at[t, p], hid_send_down.at[t, p])
    for c in range(chips):
        sent(y_pair.at[c], pair_send.at[c])

        @pl.when(c != chip)
        def _():
            sent(y_own.at[c], chip_send.at[c])


def rest(att, res, gain, pack, unpack, wo, wg, wu, wd):
    n, m = lax.axis_size("dp"), lax.axis_size("hd")
    slots, half_f = att.shape[0], att.shape[1] // 2
    nb, width = n // m, wo.shape[1]
    rows = pack.shape[0]
    features = wd.shape[1]
    units = wd.shape[0]
    tiles = 3 if units % 384 == 0 else 1
    tile = units // tiles
    quarters = 4
    chips = n // 2
    mine = rows // m
    bf, f32 = jnp.bfloat16, jnp.float32
    vmem = pl.BlockSpec(memory_space=pltpu.VMEM)
    hbm = pl.BlockSpec(memory_space=pl.ANY)
    dma = pltpu.SemaphoreType.DMA
    step_rows = rows // quarters
    scratch = [
        pltpu.VMEM(wo.shape, bf),
        pltpu.VMEM(wg.shape, bf),
        pltpu.VMEM(wu.shape, bf),
        pltpu.VMEM(wd.shape, bf),
        pltpu.VMEM((2, n, slots, half_f), bf),
        pltpu.VMEM((n * slots, width), f32),
        pltpu.VMEM((n, slots, width), bf),
        pltpu.VMEM((rows, width), bf),
        pltpu.VMEM((quarters, step_rows, width), bf),
        pltpu.VMEM((quarters, step_rows, width), bf),
        pltpu.VMEM((nb, rows, width), bf),
        pltpu.VMEM((nb, rows, width), bf),
        pltpu.VMEM((rows, 128), f32),
        pltpu.VMEM((m, mine, 128), f32),
        pltpu.VMEM((tiles, m, mine, 2 * tile), bf),
        pltpu.VMEM((2, tiles, m, mine, 2 * tile), bf),
        pltpu.VMEM((tiles, m, mine, tile), bf),
        pltpu.VMEM((rows, features), bf),
        pltpu.VMEM((chips, slots, features), bf),
        pltpu.VMEM((chips, slots, features), bf),
        pltpu.VMEM((chips, slots, features), bf),
        pltpu.VMEM((chips, slots, features), bf),
        dma((4,)),
        dma((2,)),
        dma((2, chips)),
        dma((2, chips)),
        dma((2, n)),
        dma((nb,)),
        dma((n,)),
        dma((quarters,)),
        dma((quarters,)),
        dma((quarters,)),
        dma((nb // 2, quarters)),
        dma((nb // 2, quarters)),
        dma((nb, quarters)),
        dma((m,)),
        dma((m,)),
        dma((tiles, m)),
        dma((2, tiles, m)),
        dma((tiles, m)),
        dma((tiles, m)),
        dma((tiles, m)),
        dma((chips,)),
        dma((chips,)),
        dma((chips,)),
        dma((chips,)),
    ]
    return pl.pallas_call(
        functools.partial(layer_kernel, n, m),
        out_shape=jax.ShapeDtypeStruct((slots, features), bf),
        in_specs=[vmem] * 5 + [hbm] * 4,
        out_specs=vmem,
        scratch_shapes=scratch,
        compiler_params=pltpu.CompilerParams(
            collective_id=0, has_side_effects=True, vmem_limit_bytes=60 * 1024 * 1024
        ),
        cost_estimate=pl.CostEstimate(
            flops=2 * rows * (wo.size + wg.size + wu.size + wd.size),
            bytes_accessed=2 * (wo.size + wg.size + wu.size + wd.size),
            transcendentals=0,
        ),
    )(att, res, gain, pack, unpack, wo, wg, wu, wd)


def on_device(
    query_nope,
    query_rope,
    latent,
    key_rope,
    key_up,
    value_up,
    output_weight,
    residual,
    norm_gain,
    gate_weight,
    up_weight,
    down_weight,
    rank_tokens,
    request_ids,
):
    slots = latent.shape[0]
    n, m = lax.axis_size("dp"), lax.axis_size("hd")
    nb = n // m
    attended = attend(query_nope, query_rope, latent, key_rope, key_up, value_up, request_ids[0])
    res = residual
    if output_weight.shape[1] % 128 != 0:
        res = residual.reshape(slots, nb, -1).transpose(1, 0, 2)
    gain = norm_gain.reshape(1, -1)
    rows = n * slots // 2
    first = jnp.cumsum(rank_tokens) - rank_tokens
    slot = jnp.arange(slots, dtype=jnp.int32)
    packed_row = jnp.where(
        slot[None, :] < rank_tokens[:, None], first[:, None] + slot[None, :], -1
    )
    row = jnp.arange(rows, dtype=jnp.int32)
    pack = (row[:, None] == packed_row.reshape(1, -1)).astype(jnp.bfloat16)
    unpack = (packed_row[:, :, None] == row[None, None, :]).astype(jnp.bfloat16)
    return rest(
        attended, res, gain, pack, unpack, output_weight, gate_weight, up_weight, down_weight
    )


def solution(mesh):
    in_specs = (
        P("dp", "hd"),
        P("dp", "hd"),
        P("dp", None),
        P("dp", None),
        P(None, "hd"),
        P(None, "hd"),
        P("hd", "dp"),
        P("dp", "hd"),
        P("hd"),
        P("hd", "dp"),
        P("hd", "dp"),
        P("dp", "hd"),
        P(),
        P("dp", None),
    )
    out_specs = P("dp", "hd")
    return jax.shard_map(
        on_device, mesh=mesh, in_specs=in_specs, out_specs=out_specs, check_vma=False
    )
```

```python
import functools

import jax
import jax.numpy as jnp
from jax import lax
from jax.experimental import pallas as pl
from jax.experimental.pallas import tpu as pltpu
from jax.sharding import PartitionSpec as P

NOPE = 128
ROPE = 64
VH = 128
MESH = pl.DeviceIdType.MESH


def attend(query_nope, query_rope, latent, key_rope, key_up, value_up, request_row):
    slots = latent.shape[0]
    heads = key_up.shape[1] // NOPE
    key_nope = jnp.dot(latent, key_up, preferred_element_type=jnp.float32).astype(jnp.bfloat16)
    values = jnp.dot(latent, value_up, preferred_element_type=jnp.float32).astype(jnp.bfloat16)
    query_heads = query_nope.reshape(slots, heads, NOPE)
    rotary_heads = query_rope.reshape(slots, heads, ROPE)
    scores = jnp.einsum(
        "shd,thd->hst",
        query_heads,
        key_nope.reshape(slots, heads, NOPE),
        preferred_element_type=jnp.float32,
    )
    scores = scores + jnp.einsum(
        "shd,td->hst", rotary_heads, key_rope, preferred_element_type=jnp.float32
    )
    scores = scores * (NOPE + ROPE) ** (-0.5)
    position = jnp.arange(slots, dtype=jnp.int32)
    allowed = (request_row[:, None] == request_row[None, :]) & (
        position[None, :] <= position[:, None]
    )
    scores = jnp.where(allowed[None, :, :], scores, jnp.float32(-1e30))
    top = jnp.max(scores, axis=-1, keepdims=True)
    raised = jnp.exp(scores - top)
    weights = (raised / jnp.sum(raised, axis=-1, keepdims=True)).astype(jnp.bfloat16)
    attended = jnp.einsum(
        "hst,thd->shd",
        weights,
        values.reshape(slots, heads, VH),
        preferred_element_type=jnp.float32,
    )
    return attended.astype(jnp.bfloat16).reshape(slots, heads * VH)


def f32_dot(a, b):
    return jnp.dot(a, b, preferred_element_type=jnp.float32)


def layer_kernel(
    n,
    m,
    att,
    res,
    gain,
    pack,
    unpack,
    wo_hbm,
    wg_hbm,
    wu_hbm,
    wd_hbm,
    out,
    wo,
    wg,
    wu,
    wd,
    gathered,
    acc,
    res_all,
    part,
    from_low,
    from_high,
    mixed,
    scaled,
    squares,
    squares_all,
    gu,
    gu_in,
    hidden,
    mlp,
    y,
    y_pair,
    pair_in,
    y_own,
    chip_in,
    w_sem,
    own_sem,
    ag_ring_send,
    ag_pair_send,
    ag_recv,
    res_send,
    res_recv,
    line_send,
    line_low,
    line_high,
    bc_ring_send,
    bc_pair_send,
    bc_recv,
    sq_send,
    sq_recv,
    gu_send,
    gu_recv,
    hid_send,
    hid_recv,
    pair_send,
    pair_recv,
    chip_send,
    chip_recv,
):
    i, j = lax.axis_index("dp"), lax.axis_index("hd")
    chips = n // 2
    chip, core = i // 2, lax.rem(i, 2)
    sibling = i + 1 - 2 * core
    side = 1
    while side * side < chips:
        side *= 2
    nb, rows, width = mixed.shape
    tiles = gu.shape[0]
    tile = gu.shape[3] // 2
    mine = rows // 2
    quarters = from_low.shape[0]
    step_rows = rows // quarters
    parts, half_f = gathered.shape[0], gathered.shape[3]
    turns = [h for p in range(parts // 2) for h in (p, p + parts // 2)]
    slots = att.shape[0]

    def att_half(h):
        return att.at[:, pl.ds(h * half_f, half_f)]

    def res_block(b):
        return res.at[:, pl.ds(b * width, width)] if len(res.shape) == 2 else res.at[b]

    def place(c):
        a, b = c // side, lax.rem(c, side)
        return a * side + b + lax.rem(a, 2) * (side - 1 - 2 * b)

    def chip_at(k):
        k = lax.rem(k + 2 * chips, chips)
        a, b = k // side, lax.rem(k, side)
        return a * side + b + lax.rem(a, 2) * (side - 1 - 2 * b)

    here = place(chip)
    after, before = 2 * chip_at(here + 1) + core, 2 * chip_at(here - 1) + core

    def send(src, dst, s_sem, r_sem, dp, hd):
        copy = pltpu.make_async_remote_copy(
            src_ref=src,
            dst_ref=dst,
            send_sem=s_sem,
            recv_sem=r_sem,
            device_id={"dp": dp, "hd": hd},
            device_id_type=MESH,
        )
        copy.start()

    def landed(ref, r_sem):
        pltpu.make_async_copy(ref, ref, r_sem).wait()

    loads = []
    for q, (a, b) in enumerate(((wo_hbm, wo), (wg_hbm, wg), (wu_hbm, wu), (wd_hbm, wd))):
        load = pltpu.make_async_copy(a, b, w_sem.at[q])
        if q == 0:
            load.start()
        loads.append(load)
    from_low[...] = jnp.zeros_like(from_low)
    from_high[...] = jnp.zeros_like(from_high)

    barrier = pltpu.get_barrier_semaphore()
    for d in range(1, n):
        pl.semaphore_signal(
            barrier, inc=1, device_id={"dp": lax.rem(i + d, n), "hd": j}, device_id_type=MESH
        )
    for d in range(1, m):
        pl.semaphore_signal(
            barrier, inc=1, device_id={"dp": i, "hd": lax.rem(j + d, m)}, device_id_type=MESH
        )
    pl.semaphore_wait(barrier, n + m - 2)

    for h in turns:
        send(
            att_half(h),
            gathered.at[h, i],
            ag_ring_send.at[h, 0],
            ag_recv.at[h, i],
            (after, before)[h // (parts // 2)],
            j,
        )
    for h in turns:
        send(att_half(h), gathered.at[h, i], ag_pair_send.at[h, 0], ag_recv.at[h, i], sibling, j)
        pltpu.make_async_copy(att_half(h), gathered.at[h, i], own_sem.at[h]).start()
    loads[0].wait()
    for load in loads[1:]:
        load.start()
    for step in range(chips):
        sources = [chip_at(here - step if h < parts // 2 else here + step) for h in range(parts)]
        for h in turns:
            block = 2 * sources[h] + core
            if step == 0:
                pltpu.make_async_copy(att_half(h), gathered.at[h, i], own_sem.at[h]).wait()
                continue
            landed(gathered.at[h, block], ag_recv.at[h, block])
            view = gathered.at[h, block]
            if step < chips - 1:
                send(
                    view,
                    view,
                    ag_ring_send.at[h, step],
                    ag_recv.at[h, block],
                    (after, before)[h // (parts // 2)],
                    j,
                )
            send(view, view, ag_pair_send.at[h, step], ag_recv.at[h, block], sibling, j)
        if step == chips - 1:
            for b in range(nb):
                goal = j * nb + b

                @pl.when(goal != i)
                def _():
                    send(res_block(b), res_all.at[i], res_send.at[b], res_recv.at[i], goal, j)

                @pl.when(goal == i)
                def _():
                    pltpu.make_async_copy(res_block(b), res_all.at[i], res_send.at[b]).start()

        for h in turns:
            block = 2 * sources[h] + 1 - core
            landed(gathered.at[h, block], ag_recv.at[h, block])
            both = gathered[h, pl.ds(2 * sources[h], 2)].reshape(2 * slots, half_f)
            sl = pl.ds(pl.multiple_of(2 * sources[h] * slots, 2 * slots), 2 * slots)
            term = f32_dot(both, wo[h * half_f : (h + 1) * half_f, :])
            opens = [0] if step == 0 or 2 * step == chips else [0, parts // 2]
            first = h in opens and 2 * step <= chips
            acc[sl] = term if first else acc[sl] + term
    part[...] = f32_dot(pack[...], acc[...].astype(jnp.bfloat16)).astype(jnp.bfloat16)

    target = i // nb
    slot = lax.rem(i, nb)

    def bc_forward(b, q, source_chip):
        up = q < quarters // 2
        far = lax.rem((here - place(source_chip) if up else place(source_chip) - here) + chips, chips)

        @pl.when(far < chips - 1)
        def _():
            sl = mixed.at[b, pl.ds(q * step_rows, step_rows)]
            send(sl, sl, bc_ring_send.at[b // 2, q], bc_recv.at[b, q], after if up else before, j)

    @pl.when(j == target)
    def _():
        for k in range(n):
            @pl.when(k != i)
            def _():
                landed(res_all.at[k], res_recv.at[k])

        pltpu.make_async_copy(res_all.at[i], res_all.at[i], res_send.at[slot]).wait()
        base = f32_dot(pack[...], res_all[...].reshape(n * slots, width))
        mixed[slot] = base.astype(jnp.bfloat16)

    for q in [x for p in range(quarters // 2) for x in (p, p + quarters // 2)]:
        sl = pl.ds(q * step_rows, step_rows)

        @pl.when(jnp.logical_and(j > 0, j <= target))
        def _():
            landed(from_low.at[q], line_low.at[q])

        @pl.when(jnp.logical_and(j < m - 1, j >= target))
        def _():
            landed(from_high.at[q], line_high.at[q])

        @pl.when(jnp.logical_and(j > 0, j < target))
        def _():
            part[sl] = (part[sl].astype(jnp.float32) + from_low[q].astype(jnp.float32)).astype(
                jnp.bfloat16
            )

        @pl.when(jnp.logical_and(j < m - 1, j > target))
        def _():
            part[sl] = (part[sl].astype(jnp.float32) + from_high[q].astype(jnp.float32)).astype(
                jnp.bfloat16
            )

        @pl.when(j < target)
        def _():
            send(part.at[sl], from_low.at[q], line_send.at[q], line_low.at[q], i, j + 1)

        @pl.when(j > target)
        def _():
            send(part.at[sl], from_high.at[q], line_send.at[q], line_high.at[q], i, j - 1)

        @pl.when(j == target)
        def _():
            total = mixed[slot, sl].astype(jnp.float32) + part[sl].astype(jnp.float32)
            total = total + (from_low[q].astype(jnp.float32) + from_high[q].astype(jnp.float32))
            mixed[slot, sl] = total.astype(jnp.bfloat16)
            bc_forward(slot, q, chip)
            view = mixed.at[slot, sl]
            send(view, view, bc_pair_send.at[slot // 2, q], bc_recv.at[slot, q], sibling, j)

    for q in [x for p in range(quarters // 2) for x in (p, p + quarters // 2)]:
        sl = pl.ds(q * step_rows, step_rows)
        for bb in range(nb // 2):
            b = 2 * bb + core
            source = (j * nb + b) // 2

            @pl.when(source != chip)
            def _():
                view = mixed.at[b, sl]
                landed(view, bc_recv.at[b, q])
                bc_forward(b, q, source)
                send(view, view, bc_pair_send.at[bb, q], bc_recv.at[b, q], sibling, j)

    for q in range(quarters):
        sl = pl.ds(q * step_rows, step_rows)
        for bb in range(nb // 2):
            b = 2 * bb + 1 - core
            landed(mixed.at[b, sl], bc_recv.at[b, q])

    total = jnp.zeros((rows, 1), jnp.float32)
    for b in range(nb):
        wide = mixed[b].astype(jnp.float32)
        scaled[b] = (wide * gain[:, b * width : (b + 1) * width]).astype(jnp.bfloat16)
        total = total + jnp.sum(wide * wide, axis=1, keepdims=True)
    squares[...] = jnp.broadcast_to(total, squares.shape)
    ends = (0, m - 1)
    for e in range(2):
        @pl.when(j != ends[e])
        def _():
            send(
                squares.at[pl.ds(e * mine, mine)],
                squares_all.at[j],
                sq_send.at[e],
                sq_recv.at[j],
                i,
                ends[e],
            )

    loads[1].wait()
    loads[2].wait()
    def gate_up(t):
        cols = slice(t * tile, (t + 1) * tile)
        gate = f32_dot(scaled[0], wg[:width, cols])
        up = f32_dot(scaled[0], wu[:width, cols])
        for b in range(1, nb):
            gate = gate + f32_dot(scaled[b], wg[b * width : (b + 1) * width, cols])
            up = up + f32_dot(scaled[b], wu[b * width : (b + 1) * width, cols])
        gu[t, :, :, :tile] = gate.astype(jnp.bfloat16).reshape(2, mine, tile)
        gu[t, :, :, tile:] = up.astype(jnp.bfloat16).reshape(2, mine, tile)

    def pass_sums(t):
        for turn in range(2):
            nearer = (2 * j) // m
            e = 1 - nearer if turn == 0 else nearer
            come = e * j + (1 - e) * (m - 1 - j)

            @pl.when(come < m - 1)
            def _():
                @pl.when(come > 0)
                def _():
                    landed(gu_in.at[e, t], gu_recv.at[t, e])
                    gu[t, e] = (
                        gu[t, e].astype(jnp.float32) + gu_in[e, t].astype(jnp.float32)
                    ).astype(jnp.bfloat16)

                send(
                    gu.at[t, e], gu_in.at[e, t], gu_send.at[t, e], gu_recv.at[t, e], i, j + 2 * e - 1
                )

    for t in range(tiles):
        gate_up(t)
        pass_sums(t)

    def hidden_tile(e, t):
        return hidden.at[e, :, pl.ds(t * tile, tile)]

    for e in range(2):
        @pl.when(j == ends[e])
        def _():
            square = squares[e * mine : (e + 1) * mine, :1]
            for p in range(m):
                if p != ends[e]:
                    landed(squares_all.at[p], sq_recv.at[p])
                    square = square + squares_all[p, :, :1]
            scale = lax.rsqrt(square / (m * nb * width) + 1e-06)
            for t in range(tiles):
                landed(gu_in.at[e, t], gu_recv.at[t, e])
                total = gu[t, e].astype(jnp.float32) + gu_in[e, t].astype(jnp.float32)
                gate, up = total[:, :tile] * scale, total[:, tile:] * scale
                hidden[e, :, t * tile : (t + 1) * tile] = (
                    gate / (1.0 + jnp.exp(-gate)) * up
                ).astype(jnp.bfloat16)
                send(
                    hidden_tile(e, t),
                    hidden_tile(e, t),
                    hid_send.at[t, e],
                    hid_recv.at[t, e],
                    i,
                    j + 1 - 2 * e,
                )

    loads[3].wait()
    group = 3 if tiles % 3 == 0 else 1
    for t in range(tiles):
        for turn in range(2):
            nearer = (2 * j) // m
            e = nearer if turn == 0 else 1 - nearer
            gone = (1 - e) * j + e * (m - 1 - j)

            @pl.when(gone > 0)
            def _():
                landed(hidden_tile(e, t), hid_recv.at[t, e])

                @pl.when(gone < m - 1)
                def _():
                    send(
                        hidden_tile(e, t),
                        hidden_tile(e, t),
                        hid_send.at[t, e],
                        hid_recv.at[t, e],
                        i,
                        j + 1 - 2 * e,
                    )

        if t % group == group - 1:
            units = slice((t + 1 - group) * tile, (t + 1) * tile)
            term = f32_dot(hidden[:, :, units].reshape(rows, group * tile), wd[units, :])
            if t >= group:
                term = mlp[...] + term
            if t < tiles - 1:
                mlp[...] = term
    total = term
    y[...] = total.astype(jnp.bfloat16)

    for d in range(chips):
        c = lax.rem(chip + d + 1, chips)
        y_pair[c] = f32_dot(unpack[2 * c + 1 - core], y[...]).astype(jnp.bfloat16)
        send(y_pair.at[c], pair_in.at[c], pair_send.at[c], pair_recv.at[c], sibling, j)
    for d in range(chips):
        c = lax.rem(chip + d + 1, chips)
        mine_rows = f32_dot(unpack[2 * c + core], y[...])
        landed(pair_in.at[c], pair_recv.at[c])
        y_own[c] = (mine_rows + pair_in[c].astype(jnp.float32)).astype(jnp.bfloat16)
        if d < chips - 1:
            send(
                y_own.at[c], chip_in.at[chip], chip_send.at[c], chip_recv.at[chip], 2 * c + core, j
            )
    kept = jnp.concatenate([f32_dot(unpack[i], mixed[b]) for b in range(nb)], axis=1)
    kept = kept + y_own[chip].astype(jnp.float32)
    for d in range(1, chips):
        c = lax.rem(chip + d, chips)
        landed(chip_in.at[c], chip_recv.at[c])
        kept = kept + chip_in[c].astype(jnp.float32)
    out[...] = kept.astype(jnp.bfloat16)

    def sent(ref, sem):
        pltpu.make_async_copy(ref, ref, sem).wait()

    for h in range(parts):
        for step in range(chips):
            if step < chips - 1:
                sent(gathered.at[h, 0], ag_ring_send.at[h, step])
            sent(gathered.at[h, 0], ag_pair_send.at[h, step])
    for b in range(nb):
        @pl.when(j * nb + b != i)
        def _():
            sent(res_all.at[0], res_send.at[b])
    for q in range(quarters):
        @pl.when(j != target)
        def _():
            sent(from_low.at[q], line_send.at[q])

        for bb in range(nb // 2):
            source = (j * nb + 2 * bb + core) // 2
            up = q < quarters // 2
            far = lax.rem((here - place(source) if up else place(source) - here) + chips, chips)

            @pl.when(far < chips - 1)
            def _():
                sent(from_low.at[q], bc_ring_send.at[bb, q])

            sent(from_low.at[q], bc_pair_send.at[bb, q])
    for e in range(2):
        @pl.when(j != ends[e])
        def _():
            sent(squares_all.at[0], sq_send.at[e])

        for t in range(tiles):
            @pl.when(j != ends[e])
            def _():
                sent(gu.at[t, e], gu_send.at[t, e])

            @pl.when(j != ends[1 - e])
            def _():
                sent(hidden_tile(e, t), hid_send.at[t, e])

    for c in range(chips):
        sent(y_pair.at[c], pair_send.at[c])

        @pl.when(c != chip)
        def _():
            sent(y_own.at[c], chip_send.at[c])


def rest(att, res, gain, pack, unpack, wo, wg, wu, wd):
    n, m = lax.axis_size("dp"), lax.axis_size("hd")
    parts = 4
    slots, half_f = att.shape[0], att.shape[1] // parts
    nb, width = n // m, wo.shape[1]
    rows = pack.shape[0]
    features = wd.shape[1]
    units = wd.shape[0]
    tiles = units // 256 if units % 256 == 0 else 1
    tile = units // tiles
    quarters = 8
    chips = n // 2
    mine = rows // 2
    bf, f32 = jnp.bfloat16, jnp.float32
    vmem = pl.BlockSpec(memory_space=pltpu.VMEM)
    hbm = pl.BlockSpec(memory_space=pl.ANY)
    dma = pltpu.SemaphoreType.DMA
    step_rows = rows // quarters
    scratch = [
        pltpu.VMEM(wo.shape, bf),
        pltpu.VMEM(wg.shape, bf),
        pltpu.VMEM(wu.shape, bf),
        pltpu.VMEM(wd.shape, bf),
        pltpu.VMEM((parts, n, slots, half_f), bf),
        pltpu.VMEM((n * slots, width), f32),
        pltpu.VMEM((n, slots, width), bf),
        pltpu.VMEM((rows, width), bf),
        pltpu.VMEM((quarters, step_rows, width), bf),
        pltpu.VMEM((quarters, step_rows, width), bf),
        pltpu.VMEM((nb, rows, width), bf),
        pltpu.VMEM((nb, rows, width), bf),
        pltpu.VMEM((rows, 128), f32),
        pltpu.VMEM((m, mine, 128), f32),
        pltpu.VMEM((tiles, 2, mine, 2 * tile), bf),
        pltpu.VMEM((2, tiles, mine, 2 * tile), bf),
        pltpu.VMEM((2, mine, units), bf),
        pltpu.VMEM((rows, features), f32),
        pltpu.VMEM((rows, features), bf),
        pltpu.VMEM((chips, slots, features), bf),
        pltpu.VMEM((chips, slots, features), bf),
        pltpu.VMEM((chips, slots, features), bf),
        pltpu.VMEM((chips, slots, features), bf),
        dma((4,)),
        dma((parts,)),
        dma((parts, chips)),
        dma((parts, chips)),
        dma((parts, n)),
        dma((nb,)),
        dma((n,)),
        dma((quarters,)),
        dma((quarters,)),
        dma((quarters,)),
        dma((nb // 2, quarters)),
        dma((nb // 2, quarters)),
        dma((nb, quarters)),
        dma((m,)),
        dma((m,)),
        dma((tiles, 2)),
        dma((tiles, 2)),
        dma((tiles, 2)),
        dma((tiles, 2)),
        dma((chips,)),
        dma((chips,)),
        dma((chips,)),
        dma((chips,)),
    ]
    return pl.pallas_call(
        functools.partial(layer_kernel, n, m),
        out_shape=jax.ShapeDtypeStruct((slots, features), bf),
        in_specs=[vmem] * 5 + [hbm] * 4,
        out_specs=vmem,
        scratch_shapes=scratch,
        compiler_params=pltpu.CompilerParams(
            collective_id=0, has_side_effects=True, vmem_limit_bytes=60 * 1024 * 1024
        ),
        cost_estimate=pl.CostEstimate(
            flops=2 * rows * (wo.size + wg.size + wu.size + wd.size),
            bytes_accessed=2 * (wo.size + wg.size + wu.size + wd.size),
            transcendentals=0,
        ),
    )(att, res, gain, pack, unpack, wo, wg, wu, wd)


def on_device(
    query_nope,
    query_rope,
    latent,
    key_rope,
    key_up,
    value_up,
    output_weight,
    residual,
    norm_gain,
    gate_weight,
    up_weight,
    down_weight,
    rank_tokens,
    request_ids,
):
    slots = latent.shape[0]
    n, m = lax.axis_size("dp"), lax.axis_size("hd")
    nb = n // m
    attended = attend(query_nope, query_rope, latent, key_rope, key_up, value_up, request_ids[0])
    res = residual
    if output_weight.shape[1] % 128 != 0:
        res = residual.reshape(slots, nb, -1).transpose(1, 0, 2)
    gain = norm_gain.reshape(1, -1)
    rows = n * slots // 2
    first = jnp.cumsum(rank_tokens) - rank_tokens
    slot = jnp.arange(slots, dtype=jnp.int32)
    packed_row = jnp.where(
        slot[None, :] < rank_tokens[:, None], first[:, None] + slot[None, :], -1
    )
    row = jnp.arange(rows, dtype=jnp.int32)
    pack = (row[:, None] == packed_row.reshape(1, -1)).astype(jnp.bfloat16)
    unpack = (packed_row[:, :, None] == row[None, None, :]).astype(jnp.bfloat16)
    return rest(
        attended, res, gain, pack, unpack, output_weight, gate_weight, up_weight, down_weight
    )


def solution(mesh):
    in_specs = (
        P("dp", "hd"),
        P("dp", "hd"),
        P("dp", None),
        P("dp", None),
        P(None, "hd"),
        P(None, "hd"),
        P("hd", "dp"),
        P("dp", "hd"),
        P("hd"),
        P("hd", "dp"),
        P("hd", "dp"),
        P("dp", "hd"),
        P(),
        P("dp", None),
    )
    out_specs = P("dp", "hd")
    return jax.shard_map(
        on_device, mesh=mesh, in_specs=in_specs, out_specs=out_specs, check_vma=False
    )
```

```python
import functools

import jax
import jax.numpy as jnp
from jax import lax
from jax.experimental import pallas as pl
from jax.experimental.pallas import tpu as pltpu
from jax.sharding import PartitionSpec as P

NOPE = 128
ROPE = 64
VH = 128
MESH = pl.DeviceIdType.MESH


def attend(query_nope, query_rope, latent, key_rope, key_up, value_up, request_row):
    slots = latent.shape[0]
    heads = key_up.shape[1] // NOPE
    key_nope = jnp.dot(latent, key_up, preferred_element_type=jnp.float32).astype(jnp.bfloat16)
    values = jnp.dot(latent, value_up, preferred_element_type=jnp.float32).astype(jnp.bfloat16)
    query_heads = query_nope.reshape(slots, heads, NOPE)
    rotary_heads = query_rope.reshape(slots, heads, ROPE)
    scores = jnp.einsum(
        "shd,thd->hst",
        query_heads,
        key_nope.reshape(slots, heads, NOPE),
        preferred_element_type=jnp.float32,
    )
    scores = scores + jnp.einsum(
        "shd,td->hst", rotary_heads, key_rope, preferred_element_type=jnp.float32
    )
    scores = scores * (NOPE + ROPE) ** (-0.5)
    position = jnp.arange(slots, dtype=jnp.int32)
    allowed = (request_row[:, None] == request_row[None, :]) & (
        position[None, :] <= position[:, None]
    )
    scores = jnp.where(allowed[None, :, :], scores, jnp.float32(-1e30))
    top = jnp.max(scores, axis=-1, keepdims=True)
    raised = jnp.exp(scores - top)
    weights = (raised / jnp.sum(raised, axis=-1, keepdims=True)).astype(jnp.bfloat16)
    attended = jnp.einsum(
        "hst,thd->shd",
        weights,
        values.reshape(slots, heads, VH),
        preferred_element_type=jnp.float32,
    )
    return attended.astype(jnp.bfloat16).reshape(slots, heads * VH)


def f32_dot(a, b):
    return jnp.dot(a, b, preferred_element_type=jnp.float32)


def layer_kernel(
    n,
    m,
    att,
    res,
    gain,
    pack,
    unpack,
    wo_hbm,
    wg_hbm,
    wu_hbm,
    wd_hbm,
    out,
    wo,
    wg,
    wu,
    wd,
    gathered,
    acc,
    res_all,
    part,
    from_low,
    from_high,
    mixed,
    scaled,
    squares,
    squares_all,
    gu,
    gu_in,
    hidden,
    mlp,
    y,
    y_pair,
    pair_in,
    y_own,
    chip_in,
    w_sem,
    own_sem,
    ag_ring_send,
    ag_pair_send,
    ag_recv,
    res_send,
    res_recv,
    line_send,
    line_low,
    line_high,
    bc_ring_send,
    bc_pair_send,
    bc_recv,
    sq_send,
    sq_recv,
    gu_send,
    gu_recv,
    hid_send,
    hid_recv,
    pair_send,
    pair_recv,
    chip_send,
    chip_recv,
):
    i, j = lax.axis_index("dp"), lax.axis_index("hd")
    chips = n // 2
    chip, core = i // 2, lax.rem(i, 2)
    sibling = i + 1 - 2 * core
    side = 1
    while side * side < chips:
        side *= 2
    nb, rows, width = mixed.shape
    tiles = gu.shape[0]
    tile = gu.shape[3] // 2
    mine = rows // 2
    quarters = from_low.shape[0]
    step_rows = rows // quarters
    parts, half_f = gathered.shape[0], gathered.shape[3]
    turns = [h for p in range(parts // 2) for h in (p, p + parts // 2)]
    slots = att.shape[0]

    def att_half(h):
        return att.at[:, pl.ds(h * half_f, half_f)]

    def res_block(b):
        return res.at[:, pl.ds(b * width, width)] if len(res.shape) == 2 else res.at[b]

    def place(c):
        a, b = c // side, lax.rem(c, side)
        return a * side + b + lax.rem(a, 2) * (side - 1 - 2 * b)

    def chip_at(k):
        k = lax.rem(k + 2 * chips, chips)
        a, b = k // side, lax.rem(k, side)
        return a * side + b + lax.rem(a, 2) * (side - 1 - 2 * b)

    here = place(chip)
    after, before = 2 * chip_at(here + 1) + core, 2 * chip_at(here - 1) + core

    def send(src, dst, s_sem, r_sem, dp, hd):
        copy = pltpu.make_async_remote_copy(
            src_ref=src,
            dst_ref=dst,
            send_sem=s_sem,
            recv_sem=r_sem,
            device_id={"dp": dp, "hd": hd},
            device_id_type=MESH,
        )
        copy.start()

    def landed(ref, r_sem):
        pltpu.make_async_copy(ref, ref, r_sem).wait()

    loads = []
    for q, (a, b) in enumerate(((wo_hbm, wo), (wg_hbm, wg), (wu_hbm, wu), (wd_hbm, wd))):
        load = pltpu.make_async_copy(a, b, w_sem.at[q])
        if q == 0:
            load.start()
        loads.append(load)
    from_low[...] = jnp.zeros_like(from_low)
    from_high[...] = jnp.zeros_like(from_high)

    barrier = pltpu.get_barrier_semaphore()
    for d in range(1, n):
        pl.semaphore_signal(
            barrier, inc=1, device_id={"dp": lax.rem(i + d, n), "hd": j}, device_id_type=MESH
        )
    for d in range(1, m):
        pl.semaphore_signal(
            barrier, inc=1, device_id={"dp": i, "hd": lax.rem(j + d, m)}, device_id_type=MESH
        )
    pl.semaphore_wait(barrier, n + m - 2)

    for h in turns:
        send(
            att_half(h),
            gathered.at[h, i],
            ag_ring_send.at[h, 0],
            ag_recv.at[h, i],
            (after, before)[h // (parts // 2)],
            j,
        )
    for h in turns:
        send(att_half(h), gathered.at[h, i], ag_pair_send.at[h, 0], ag_recv.at[h, i], sibling, j)
        pltpu.make_async_copy(att_half(h), gathered.at[h, i], own_sem.at[h]).start()
    loads[0].wait()
    for load in loads[1:]:
        load.start()
    for step in range(chips):
        sources = [chip_at(here - step if h < parts // 2 else here + step) for h in range(parts)]
        for h in turns:
            block = 2 * sources[h] + core
            if step == 0:
                pltpu.make_async_copy(att_half(h), gathered.at[h, i], own_sem.at[h]).wait()
                continue
            landed(gathered.at[h, block], ag_recv.at[h, block])
            view = gathered.at[h, block]
            if step < chips - 1:
                send(
                    view,
                    view,
                    ag_ring_send.at[h, step],
                    ag_recv.at[h, block],
                    (after, before)[h // (parts // 2)],
                    j,
                )
            send(view, view, ag_pair_send.at[h, step], ag_recv.at[h, block], sibling, j)
        if step == chips - 1:
            for b in range(nb):
                goal = j * nb + b

                @pl.when(goal != i)
                def _():
                    send(res_block(b), res_all.at[i], res_send.at[b], res_recv.at[i], goal, j)

                @pl.when(goal == i)
                def _():
                    pltpu.make_async_copy(res_block(b), res_all.at[i], res_send.at[b]).start()

        for h in turns:
            block = 2 * sources[h] + 1 - core
            landed(gathered.at[h, block], ag_recv.at[h, block])
            both = gathered[h, pl.ds(2 * sources[h], 2)].reshape(2 * slots, half_f)
            sl = pl.ds(pl.multiple_of(2 * sources[h] * slots, 2 * slots), 2 * slots)
            term = f32_dot(both, wo[h * half_f : (h + 1) * half_f, :])
            opens = [0] if step == 0 or 2 * step == chips else [0, parts // 2]
            first = h in opens and 2 * step <= chips
            acc[sl] = term if first else acc[sl] + term
    part[...] = f32_dot(pack[...], acc[...].astype(jnp.bfloat16)).astype(jnp.bfloat16)

    target = i // nb
    slot = lax.rem(i, nb)

    def ring_far(way, source_chip):
        up = here - place(source_chip)
        return lax.rem((1 - 2 * way) * up + chips, chips)

    def row_chunk(q):
        return pl.ds(pl.multiple_of(q * step_rows, step_rows), step_rows)

    def bc_forward(b, q, way, source_chip):
        onward = (1 - way) * after + way * before

        @pl.when(ring_far(way, source_chip) < chips - 1)
        def _():
            view = mixed.at[b, row_chunk(q)]
            send(view, view, bc_ring_send.at[b // 2, q], bc_recv.at[b, q], onward, j)

    @pl.when(j == target)
    def _():
        for k in range(n):
            @pl.when(k != i)
            def _():
                landed(res_all.at[k], res_recv.at[k])

        pltpu.make_async_copy(res_all.at[i], res_all.at[i], res_send.at[slot]).wait()
        base = f32_dot(pack[...], res_all[...].reshape(n * slots, width))
        mixed[slot] = base.astype(jnp.bfloat16)

    for q in [x for p in range(quarters // 2) for x in (p, p + quarters // 2)]:
        sl = pl.ds(q * step_rows, step_rows)

        @pl.when(jnp.logical_and(j > 0, j <= target))
        def _():
            landed(from_low.at[q], line_low.at[q])

        @pl.when(jnp.logical_and(j < m - 1, j >= target))
        def _():
            landed(from_high.at[q], line_high.at[q])

        @pl.when(jnp.logical_and(j > 0, j < target))
        def _():
            part[sl] = (part[sl].astype(jnp.float32) + from_low[q].astype(jnp.float32)).astype(
                jnp.bfloat16
            )

        @pl.when(jnp.logical_and(j < m - 1, j > target))
        def _():
            part[sl] = (part[sl].astype(jnp.float32) + from_high[q].astype(jnp.float32)).astype(
                jnp.bfloat16
            )

        @pl.when(j < target)
        def _():
            send(part.at[sl], from_low.at[q], line_send.at[q], line_low.at[q], i, j + 1)

        @pl.when(j > target)
        def _():
            send(part.at[sl], from_high.at[q], line_send.at[q], line_high.at[q], i, j - 1)

        @pl.when(j == target)
        def _():
            total = mixed[slot, sl].astype(jnp.float32) + part[sl].astype(jnp.float32)
            total = total + (from_low[q].astype(jnp.float32) + from_high[q].astype(jnp.float32))
            mixed[slot, sl] = total.astype(jnp.bfloat16)
            bc_forward(slot, q, q // (quarters // 2), chip)
            view = mixed.at[slot, sl]
            send(view, view, bc_pair_send.at[slot // 2, q], bc_recv.at[slot, q], sibling, j)

    lag = 2
    for x in range(quarters // 2 + lag):
        for bb in range(nb // 2):
            b = 2 * bb + core
            source = (j * nb + b) // 2
            nearer = (2 * ring_far(0, source)) // (chips + 1)
            for turn in range(2):
                p = x - lag * turn
                if not 0 <= p < quarters // 2:
                    continue
                way = nearer if turn == 0 else 1 - nearer
                q = way * (quarters // 2) + p

                @pl.when(source != chip)
                def _():
                    view = mixed.at[b, row_chunk(q)]
                    landed(view, bc_recv.at[b, q])
                    bc_forward(b, q, way, source)
                    send(view, view, bc_pair_send.at[bb, q], bc_recv.at[b, q], sibling, j)

    for q in range(quarters):
        sl = pl.ds(q * step_rows, step_rows)
        for bb in range(nb // 2):
            b = 2 * bb + 1 - core
            landed(mixed.at[b, sl], bc_recv.at[b, q])

    total = jnp.zeros((rows, 1), jnp.float32)
    for b in range(nb):
        wide = mixed[b].astype(jnp.float32)
        scaled[b] = (wide * gain[:, b * width : (b + 1) * width]).astype(jnp.bfloat16)
        total = total + jnp.sum(wide * wide, axis=1, keepdims=True)
    squares[...] = jnp.broadcast_to(total, squares.shape)
    ends = (0, m - 1)
    for e in range(2):
        @pl.when(j != ends[e])
        def _():
            send(
                squares.at[pl.ds(e * mine, mine)],
                squares_all.at[j],
                sq_send.at[e],
                sq_recv.at[j],
                i,
                ends[e],
            )

    loads[1].wait()
    loads[2].wait()
    def gate_up(t):
        cols = slice(t * tile, (t + 1) * tile)
        gate = f32_dot(scaled[0], wg[:width, cols])
        up = f32_dot(scaled[0], wu[:width, cols])
        for b in range(1, nb):
            gate = gate + f32_dot(scaled[b], wg[b * width : (b + 1) * width, cols])
            up = up + f32_dot(scaled[b], wu[b * width : (b + 1) * width, cols])
        gu[t, :, :, :tile] = gate.astype(jnp.bfloat16).reshape(2, mine, tile)
        gu[t, :, :, tile:] = up.astype(jnp.bfloat16).reshape(2, mine, tile)

    nearer = (2 * j) // m

    def pass_sums(t, e):
        come = e * j + (1 - e) * (m - 1 - j)

        @pl.when(come < m - 1)
        def _():
            @pl.when(come > 0)
            def _():
                landed(gu_in.at[e, t], gu_recv.at[t, e])
                gu[t, e] = (
                    gu[t, e].astype(jnp.float32) + gu_in[e, t].astype(jnp.float32)
                ).astype(jnp.bfloat16)

            send(gu.at[t, e], gu_in.at[e, t], gu_send.at[t, e], gu_recv.at[t, e], i, j + 2 * e - 1)

    for t in range(tiles + lag):
        if t < tiles:
            gate_up(t)
            pass_sums(t, 1 - nearer)
        if t >= lag:
            pass_sums(t - lag, nearer)

    def hidden_tile(e, t):
        return hidden.at[e, :, pl.ds(t * tile, tile)]

    for e in range(2):
        @pl.when(j == ends[e])
        def _():
            square = squares[e * mine : (e + 1) * mine, :1]
            for p in range(m):
                if p != ends[e]:
                    landed(squares_all.at[p], sq_recv.at[p])
                    square = square + squares_all[p, :, :1]
            scale = lax.rsqrt(square / (m * nb * width) + 1e-06)
            for t in range(tiles):
                landed(gu_in.at[e, t], gu_recv.at[t, e])
                total = gu[t, e].astype(jnp.float32) + gu_in[e, t].astype(jnp.float32)
                gate, up = total[:, :tile] * scale, total[:, tile:] * scale
                hidden[e, :, t * tile : (t + 1) * tile] = (
                    gate / (1.0 + jnp.exp(-gate)) * up
                ).astype(jnp.bfloat16)
                send(
                    hidden_tile(e, t),
                    hidden_tile(e, t),
                    hid_send.at[t, e],
                    hid_recv.at[t, e],
                    i,
                    j + 1 - 2 * e,
                )

    loads[3].wait()
    group = 3 if tiles % 3 == 0 else 1
    def pass_hidden(t, e):
        gone = (1 - e) * j + e * (m - 1 - j)

        @pl.when(gone > 0)
        def _():
            landed(hidden_tile(e, t), hid_recv.at[t, e])

            @pl.when(gone < m - 1)
            def _():
                send(
                    hidden_tile(e, t),
                    hidden_tile(e, t),
                    hid_send.at[t, e],
                    hid_recv.at[t, e],
                    i,
                    j + 1 - 2 * e,
                )

    for x in range(tiles + lag):
        if x < tiles:
            pass_hidden(x, nearer)
        t = x - lag
        if t < 0:
            continue
        pass_hidden(t, 1 - nearer)
        if t % group == group - 1:
            units = slice((t + 1 - group) * tile, (t + 1) * tile)
            term = f32_dot(hidden[:, :, units].reshape(rows, group * tile), wd[units, :])
            if t >= group:
                term = mlp[...] + term
            if t < tiles - 1:
                mlp[...] = term
    total = term
    y[...] = total.astype(jnp.bfloat16)

    for d in range(chips):
        c = lax.rem(chip + d + 1, chips)
        y_pair[c] = f32_dot(unpack[2 * c + 1 - core], y[...]).astype(jnp.bfloat16)
        send(y_pair.at[c], pair_in.at[c], pair_send.at[c], pair_recv.at[c], sibling, j)
    for d in range(chips):
        c = lax.rem(chip + d + 1, chips)
        mine_rows = f32_dot(unpack[2 * c + core], y[...])
        landed(pair_in.at[c], pair_recv.at[c])
        y_own[c] = (mine_rows + pair_in[c].astype(jnp.float32)).astype(jnp.bfloat16)
        if d < chips - 1:
            send(
                y_own.at[c], chip_in.at[chip], chip_send.at[c], chip_recv.at[chip], 2 * c + core, j
            )
    kept = jnp.concatenate([f32_dot(unpack[i], mixed[b]) for b in range(nb)], axis=1)
    kept = kept + y_own[chip].astype(jnp.float32)
    for d in range(1, chips):
        c = lax.rem(chip + d, chips)
        landed(chip_in.at[c], chip_recv.at[c])
        kept = kept + chip_in[c].astype(jnp.float32)
    out[...] = kept.astype(jnp.bfloat16)

    def sent(ref, sem):
        pltpu.make_async_copy(ref, ref, sem).wait()

    for h in range(parts):
        for step in range(chips):
            if step < chips - 1:
                sent(gathered.at[h, 0], ag_ring_send.at[h, step])
            sent(gathered.at[h, 0], ag_pair_send.at[h, step])
    for b in range(nb):
        @pl.when(j * nb + b != i)
        def _():
            sent(res_all.at[0], res_send.at[b])
    for q in range(quarters):
        @pl.when(j != target)
        def _():
            sent(from_low.at[q], line_send.at[q])

        for bb in range(nb // 2):
            source = (j * nb + 2 * bb + core) // 2
            @pl.when(ring_far(q // (quarters // 2), source) < chips - 1)
            def _():
                sent(from_low.at[q], bc_ring_send.at[bb, q])

            sent(from_low.at[q], bc_pair_send.at[bb, q])
    for e in range(2):
        @pl.when(j != ends[e])
        def _():
            sent(squares_all.at[0], sq_send.at[e])

        for t in range(tiles):
            @pl.when(j != ends[e])
            def _():
                sent(gu.at[t, e], gu_send.at[t, e])

            @pl.when(j != ends[1 - e])
            def _():
                sent(hidden_tile(e, t), hid_send.at[t, e])

    for c in range(chips):
        sent(y_pair.at[c], pair_send.at[c])

        @pl.when(c != chip)
        def _():
            sent(y_own.at[c], chip_send.at[c])


def rest(att, res, gain, pack, unpack, wo, wg, wu, wd):
    n, m = lax.axis_size("dp"), lax.axis_size("hd")
    parts = 4
    slots, half_f = att.shape[0], att.shape[1] // parts
    nb, width = n // m, wo.shape[1]
    rows = pack.shape[0]
    features = wd.shape[1]
    units = wd.shape[0]
    tiles = units // 256 if units % 256 == 0 else 1
    tile = units // tiles
    quarters = 8
    chips = n // 2
    mine = rows // 2
    bf, f32 = jnp.bfloat16, jnp.float32
    vmem = pl.BlockSpec(memory_space=pltpu.VMEM)
    hbm = pl.BlockSpec(memory_space=pl.ANY)
    dma = pltpu.SemaphoreType.DMA
    step_rows = rows // quarters
    scratch = [
        pltpu.VMEM(wo.shape, bf),
        pltpu.VMEM(wg.shape, bf),
        pltpu.VMEM(wu.shape, bf),
        pltpu.VMEM(wd.shape, bf),
        pltpu.VMEM((parts, n, slots, half_f), bf),
        pltpu.VMEM((n * slots, width), f32),
        pltpu.VMEM((n, slots, width), bf),
        pltpu.VMEM((rows, width), bf),
        pltpu.VMEM((quarters, step_rows, width), bf),
        pltpu.VMEM((quarters, step_rows, width), bf),
        pltpu.VMEM((nb, rows, width), bf),
        pltpu.VMEM((nb, rows, width), bf),
        pltpu.VMEM((rows, 128), f32),
        pltpu.VMEM((m, mine, 128), f32),
        pltpu.VMEM((tiles, 2, mine, 2 * tile), bf),
        pltpu.VMEM((2, tiles, mine, 2 * tile), bf),
        pltpu.VMEM((2, mine, units), bf),
        pltpu.VMEM((rows, features), f32),
        pltpu.VMEM((rows, features), bf),
        pltpu.VMEM((chips, slots, features), bf),
        pltpu.VMEM((chips, slots, features), bf),
        pltpu.VMEM((chips, slots, features), bf),
        pltpu.VMEM((chips, slots, features), bf),
        dma((4,)),
        dma((parts,)),
        dma((parts, chips)),
        dma((parts, chips)),
        dma((parts, n)),
        dma((nb,)),
        dma((n,)),
        dma((quarters,)),
        dma((quarters,)),
        dma((quarters,)),
        dma((nb // 2, quarters)),
        dma((nb // 2, quarters)),
        dma((nb, quarters)),
        dma((m,)),
        dma((m,)),
        dma((tiles, 2)),
        dma((tiles, 2)),
        dma((tiles, 2)),
        dma((tiles, 2)),
        dma((chips,)),
        dma((chips,)),
        dma((chips,)),
        dma((chips,)),
    ]
    return pl.pallas_call(
        functools.partial(layer_kernel, n, m),
        out_shape=jax.ShapeDtypeStruct((slots, features), bf),
        in_specs=[vmem] * 5 + [hbm] * 4,
        out_specs=vmem,
        scratch_shapes=scratch,
        compiler_params=pltpu.CompilerParams(
            collective_id=0, has_side_effects=True, vmem_limit_bytes=60 * 1024 * 1024
        ),
        cost_estimate=pl.CostEstimate(
            flops=2 * rows * (wo.size + wg.size + wu.size + wd.size),
            bytes_accessed=2 * (wo.size + wg.size + wu.size + wd.size),
            transcendentals=0,
        ),
    )(att, res, gain, pack, unpack, wo, wg, wu, wd)


def on_device(
    query_nope,
    query_rope,
    latent,
    key_rope,
    key_up,
    value_up,
    output_weight,
    residual,
    norm_gain,
    gate_weight,
    up_weight,
    down_weight,
    rank_tokens,
    request_ids,
):
    slots = latent.shape[0]
    n, m = lax.axis_size("dp"), lax.axis_size("hd")
    nb = n // m
    attended = attend(query_nope, query_rope, latent, key_rope, key_up, value_up, request_ids[0])
    res = residual
    if output_weight.shape[1] % 128 != 0:
        res = residual.reshape(slots, nb, -1).transpose(1, 0, 2)
    gain = norm_gain.reshape(1, -1)
    rows = n * slots // 2
    first = jnp.cumsum(rank_tokens) - rank_tokens
    slot = jnp.arange(slots, dtype=jnp.int32)
    packed_row = jnp.where(
        slot[None, :] < rank_tokens[:, None], first[:, None] + slot[None, :], -1
    )
    row = jnp.arange(rows, dtype=jnp.int32)
    pack = (row[:, None] == packed_row.reshape(1, -1)).astype(jnp.bfloat16)
    unpack = (packed_row[:, :, None] == row[None, None, :]).astype(jnp.bfloat16)
    return rest(
        attended, res, gain, pack, unpack, output_weight, gate_weight, up_weight, down_weight
    )


def solution(mesh):
    in_specs = (
        P("dp", "hd"),
        P("dp", "hd"),
        P("dp", None),
        P("dp", None),
        P(None, "hd"),
        P(None, "hd"),
        P("hd", "dp"),
        P("dp", "hd"),
        P("hd"),
        P("hd", "dp"),
        P("hd", "dp"),
        P("dp", "hd"),
        P(),
        P("dp", None),
    )
    out_specs = P("dp", "hd")
    return jax.shard_map(
        on_device, mesh=mesh, in_specs=in_specs, out_specs=out_specs, check_vma=False
    )
```
